32 devices in a mesh: group: 16 (over z, y, core), inner: 2 (over x).
Axes of the slice: x: 2, y: 2, z: 4, core: 2. Of those that a mesh axis runs over, the one named last changes fastest.
Arguments:
- tokens: bfloat16 [16384, 768], P(('group', 'inner')), may hold values from -6 to 6
- cotangent: bfloat16 [16384, 768], P(('group', 'inner')), may hold values from -6 to 6
- segments: int32 [32, 512], P(('group', 'inner')), may hold values from 0 to 7, never falling along the last dimension, each value on 1 to 256 neighbouring positions
- w_qkv: bfloat16 [3, 768, 768], P(None, 'group', 'inner'), may hold values from -0.21875 to 0.21875
- w_out: bfloat16 [768, 768], P('group', 'inner'), may hold values from -1.75 to 1.75
- w_up: bfloat16 [768, 3072], P('group', 'inner'), may hold values from -0.21875 to 0.21875
- w_down: bfloat16 [3072, 768], P('inner', 'group'), may hold values from -0.109375 to 0.109375
- rel_embed: bfloat16 [512, 768], P('group', 'inner'), may hold values from -6 to 6
- attn_bias: bfloat16 [4, 768], replicated, may hold values from -3 to 3
- up_bias: bfloat16 [3072], replicated, may hold values from -3 to 3
- down_bias: bfloat16 [768], replicated, may hold values from -3 to 3
- norm_gain: bfloat16 [2, 768], replicated, may hold values from 0.5 to 1.5
- norm_bias: bfloat16 [2, 768], replicated, may hold values from -3 to 3
- attn_p: float32 [768, 4, 12], replicated, may hold values from -1.75 to 1.75
- attn_q: float32 [768, 4, 12], replicated, may hold values from -0.21875 to 0.21875
- up_p: float32 [3072, 12], replicated, may hold values from -1.75 to 1.75
- up_q: float32 [768, 12], replicated, may hold values from -0.21875 to 0.21875
- down_p: float32 [768, 12], replicated, may hold values from -1.75 to 1.75
- down_q: float32 [3072, 12], replicated, may hold values from -0.109375 to 0.109375
- lam: float32 [6, 12], replicated, may hold values from -3 to 3
Outputs:
- layer_out: bfloat16 [16384, 768], P(('group', 'inner'))
- grad_tokens: bfloat16 [16384, 768], P(('group', 'inner'))
- grad_attn_p: float32 [768, 4, 12], P('inner')
- grad_attn_q: float32 [768, 4, 12], P('inner')
- grad_up_p: float32 [3072, 12], P('inner')
- grad_up_q: float32 [768, 12], P('inner')
- grad_down_p: float32 [768, 12], P('inner')
- grad_down_q: float32 [3072, 12], P('inner')
- grad_lam: float32 [6, 12], replicated
The draws below stay inside these ranges and needn't reach their ends.
Inputs may be any that keep to these rules, and one draw needn't show every extreme that they name: `segments`: within each packed row segment numbers never fall, every document has at most 256 tokens and some document has exactly that many.
All inputs are finite; a program needn't handle non-finite values.
Results may differ from the reference program's by a relative error of at most 0.02.
The reference program's roundings to bfloat16 on the way count: a program that leaves them out, or rounds other values in their place, can miss the bound.
Values may be sent and summed in bfloat16 or wider, within the bound.
A program may use at most 256 MiB of HBM per device.

```python
import math
import jax
import jax.numpy as jnp
import numpy as np
from jax import lax

D = 768
H = 12
DH = 64
FF = 3072
SPAN = 256
R = 12
L = 512
SEQS = 32
TOKENS = 16384


def levels(own_key, shape, shards, least, top_value):
    factor_of = 1.0
    for dim, blocks in shards:
        steps = jax.random.uniform(jax.random.fold_in(jax.random.fold_in(own_key, 6), dim), (blocks,), jnp.float32, least / len(shards), top_value / len(shards))
        factor_of = factor_of * jnp.repeat(jnp.exp(steps), shape[dim] // blocks).reshape((-1,) + (1,) * (len(shape) - 1 - dim))
    return factor_of


def split_up(amount, total, reach, slope):
    loads = [(1 << 20) // math.isqrt(grade ** slope) + 1 for grade in range(2, amount + 1)]
    surplus, counts = total - reach - (amount - 1), [1] * (amount - 1)
    while surplus > 0:
        movable = [i for i in range(amount - 1) if counts[i] < reach]
        whole, left = sum([loads[i] for i in movable]), surplus
        for i in movable:
            extra = min(reach - counts[i], max(1, left * loads[i] // whole), surplus)
            counts[i] = counts[i] + extra
            surplus = surplus - extra
    return np.array([reach] + counts)


def ragged(own_key, amount, total, most, skew):
    if amount == 2:
        one = jax.random.randint(own_key, (), max(1, total - most), min(most, total - 1) + 1)
        return jnp.stack([one, total - one])
    lengths = jnp.asarray(split_up(amount, total, most, skew), jnp.int32)
    pairs = (amount - 1) // 2
    giver, receiver = lengths[1:1 + 2 * pairs:2], lengths[2:2 + 2 * pairs:2]
    room = jnp.minimum(giver - 1, most - receiver)
    shifted = jax.random.randint(jax.random.fold_in(own_key, 1), (pairs,), 0, 1 << 20) % (room + 1)
    lengths = lengths.at[1:1 + 2 * pairs:2].set(giver - shifted).at[2:2 + 2 * pairs:2].set(receiver + shifted)
    return lengths[jax.random.permutation(jax.random.fold_in(own_key, 2), amount)]


def centred(rng, dims, deviation, reach, cuts=(), kind=jnp.bfloat16):
    entries = jax.random.normal(rng, dims, jnp.float32) * deviation
    if len(cuts) > 0:
        entries = levels(rng, dims, cuts, -0.22, 0.18) * entries
    return jnp.clip(entries, min=-reach, max=reach).astype(kind)


def setup_inputs(seed: int = 0) -> dict:
    seeds = jax.random.split(jax.random.key(seed), 21)
    return {
        "tokens": centred(seeds[0], (TOKENS, D), 1.0, 6.0, ((0, 32),)),
        "cotangent": centred(seeds[1], (TOKENS, D), 1.0, 6.0, ((0, 32),)),
        "segments": jax.vmap(lambda own: jnp.searchsorted(jnp.cumsum(ragged(own, 8, L, L // 2, 1)), jnp.arange(L), side="right"))(jax.random.split(seeds[2], SEQS)).reshape((SEQS, L)).astype(jnp.int32),
        "w_qkv": centred(seeds[3], (3, D, D), D ** -0.5, 0.21875, ((1, 16), (2, 2))),
        "w_out": centred(seeds[4], (D, D), (D // 64) ** -0.5, 1.75, ((0, 16), (1, 2))),
        "w_up": centred(seeds[5], (D, FF), D ** -0.5, 0.21875, ((0, 16), (1, 2))),
        "w_down": centred(seeds[6], (FF, D), FF ** -0.5, 0.109375, ((0, 2), (1, 16))),
        "rel_embed": centred(seeds[7], (2 * SPAN, D), 1.0, 6.0, ((0, 16), (1, 2))),
        "attn_bias": centred(seeds[8], (4, D), 0.5, 3.0),
        "up_bias": centred(seeds[9], (FF,), 0.5, 3.0),
        "down_bias": centred(seeds[10], (D,), 0.5, 3.0),
        "norm_gain": jnp.clip(1.0 + 0.1 * jax.random.normal(seeds[11], (2, D), jnp.float32), 0.5, 1.5).astype(jnp.bfloat16),
        "norm_bias": centred(seeds[12], (2, D), 0.5, 3.0),
        "attn_p": centred(seeds[13], (D, 4, R), R ** -0.5, 1.75, (), jnp.float32),
        "attn_q": centred(seeds[14], (D, 4, R), D ** -0.5, 0.21875, (), jnp.float32),
        "up_p": centred(seeds[15], (FF, R), R ** -0.5, 1.75, (), jnp.float32),
        "up_q": centred(seeds[16], (D, R), D ** -0.5, 0.21875, (), jnp.float32),
        "down_p": centred(seeds[17], (D, R), R ** -0.5, 1.75, (), jnp.float32),
        "down_q": centred(seeds[18], (FF, R), FF ** -0.5, 0.109375, (), jnp.float32),
        "lam": centred(seeds[19], (6, R), 1.0, 3.0, (), jnp.float32),
    }


@jax.custom_vjp
def low(v):
    return lax.optimization_barrier(v.astype(jnp.bfloat16)).astype(jnp.float32)

@jax.custom_vjp
def low_back(v):
    return v

def low_keep(v):
    return (low(v), None)

def low_pass(kept, grad):
    return (grad,)

def back_keep(v):
    return (v, None)

def back_low(kept, grad):
    return (low(grad),)
low.defvjp(low_keep, low_pass)
low_back.defvjp(back_keep, back_low)
eps_norm = 1e-07
highest = lax.Precision.HIGHEST

def bucket_index(length, span_size):
    offsets = np.arange(length)[:, None] - np.arange(length)[None, :]
    middle = span_size // 2
    magnitude = np.abs(offsets)
    inside = magnitude <= middle
    clipped = np.maximum(magnitude, middle) * 1.0
    logged = np.ceil(np.log(clipped / middle) / np.log((2 * span_size - 1) / middle) * (middle - 1)) + middle
    bucket = np.where(inside, offsets, np.sign(offsets) * logged.astype(np.int32))
    return np.clip(bucket + span_size, 0, 2 * span_size - 1).astype(np.int32)

def product(factor_one, factor_two):
    return jnp.dot(factor_one, factor_two, precision=highest, preferred_element_type=jnp.float32)

def adapted(inputs, weight, bias_vec, p_factor, q_factor, scale_vec, grad_low):
    reduced = product(inputs, low(q_factor))
    if grad_low:
        reduced = low_back(reduced)
    mixed_rows = low(reduced * scale_vec)
    return product(inputs, weight) + bias_vec + product(mixed_rows, low(p_factor).T)

def layer_norm(values, gain_vec, bias_vec):
    centre = values - lax.optimization_barrier(jnp.mean(values, axis=-1, keepdims=True))
    spread = lax.optimization_barrier(jnp.mean(centre * centre, axis=-1, keepdims=True))
    return centre * lax.rsqrt(spread + eps_norm) * gain_vec + bias_vec

def layer_block(rows, seg_block, frozen, adapters, pos_query, pos_key, bucket_map):
    w_qkv, w_out, w_up, w_down, attn_bias, up_bias, down_bias, norm_gain, norm_bias = frozen
    attn_p, attn_q, up_p, up_q, down_p, down_q, lam = adapters
    seq_count = seg_block.shape[0]
    score_scale = (3.0 * DH) ** (-0.5)
    head_list = []
    for proj_num in range(3):
        projected = adapted(rows, w_qkv[proj_num], attn_bias[proj_num], attn_p[:, proj_num], attn_q[:, proj_num], lam[proj_num], True)
        head_list.append(low_back(low(projected)).reshape(seq_count, L, H, DH))
    queries, key_rows, values = head_list
    content = jnp.einsum('bihd,bjhd->bhij', queries, key_rows, precision=highest)
    to_pos = low_back(jnp.einsum('bihd,rhd->bhir', queries, pos_key.reshape(2 * SPAN, H, DH), precision=highest))
    from_pos = low_back(jnp.einsum('bjhd,rhd->bhjr', key_rows, pos_query.reshape(2 * SPAN, H, DH), precision=highest))
    grid_shape = (seq_count, H, L, L)
    near_term = jnp.take_along_axis(to_pos, jnp.broadcast_to(bucket_map, grid_shape), axis=3)
    far_term = jnp.swapaxes(jnp.take_along_axis(from_pos, jnp.broadcast_to(bucket_map.T, grid_shape), axis=3), 2, 3)
    scores = low_back((content + near_term + far_term) * score_scale)
    same_doc = seg_block[:, None, :, None] == seg_block[:, None, None, :]
    attn_probs = jax.nn.softmax(jnp.where(same_doc, scores, -1000000000.0), axis=-1)
    context = jnp.einsum('bhij,bjhd->bihd', low(attn_probs), values, precision=highest).reshape(-1, D)
    context = low_back(low(context))
    attn_out = low_back(adapted(context, w_out, attn_bias[3], attn_p[:, 3], attn_q[:, 3], lam[3], True))
    hidden = layer_norm(rows + attn_out, norm_gain[0], norm_bias[0])
    pre_act = low_back(adapted(low(hidden), w_up, up_bias, up_p, up_q, lam[4], True))
    active = low(jax.nn.gelu(pre_act, approximate=False))
    branch = low_back(adapted(active, w_down, down_bias, down_p, down_q, lam[5], True))
    return layer_norm(hidden + branch, norm_gain[1], norm_bias[1])

def reference(tokens, cotangent, segments, w_qkv, w_out, w_up, w_down, rel_embed, attn_bias, up_bias, down_bias, norm_gain, norm_bias, attn_p, attn_q, up_p, up_q, down_p, down_q, lam):
    bucket_map = jnp.asarray(bucket_index(L, SPAN))
    frozen = tuple((member.astype(jnp.float32) for member in (w_qkv, w_out, w_up, w_down, attn_bias, up_bias, down_bias, norm_gain, norm_bias)))
    embed_rows = rel_embed.astype(jnp.float32)
    seg_blocks = segments.reshape(-1, 4, L)
    run_block = jax.checkpoint(layer_block)

    def whole_layer(inputs, adapters):
        pos_query = low(adapted(embed_rows, frozen[0][0], frozen[4][0], adapters[0][:, 0], adapters[1][:, 0], adapters[6][0], False))
        pos_key = low(adapted(embed_rows, frozen[0][1], frozen[4][1], adapters[0][:, 1], adapters[1][:, 1], adapters[6][1], False))

        def scan_step(carried, block_pair):
            return (carried, run_block(block_pair[0], block_pair[1], frozen, adapters, pos_query, pos_key, bucket_map))
        unused, outputs = lax.scan(scan_step, jnp.zeros((), jnp.float32), (inputs.reshape(-1, 4 * L, D), seg_blocks))
        return outputs.reshape(-1, D)
    adapters_in = (attn_p, attn_q, up_p, up_q, down_p, down_q, lam)
    result, pullback = jax.vjp(whole_layer, tokens.astype(jnp.float32), adapters_in)
    grad_in, grad_adapters = pullback(cotangent.astype(jnp.float32))
    return (result.astype(jnp.bfloat16), grad_in.astype(jnp.bfloat16), grad_adapters[0], grad_adapters[1], grad_adapters[2], grad_adapters[3], grad_adapters[4], grad_adapters[5], grad_adapters[6])
```

```python
import functools

import jax
import jax.numpy as jnp
import numpy as np
from jax import lax
from jax.experimental import pallas as pl
from jax.experimental.pallas import tpu as pltpu
from jax.sharding import PartitionSpec as P

D = 768
H = 12
DH = 64
FF = 3072
SPAN = 256
L = 512
R = 12
HALF = L // 2
SCALE = (3.0 * DH) ** (-0.5)
EPS = 1e-07

bf16 = jnp.bfloat16
f32 = jnp.float32


def bucket_values(offsets, span_size):
    middle = span_size // 2
    magnitude = np.abs(offsets)
    inside = magnitude <= middle
    clipped = np.maximum(magnitude, middle) * 1.0
    logged = (
        np.ceil(np.log(clipped / middle) / np.log((2 * span_size - 1) / middle) * (middle - 1))
        + middle
    )
    bucket = np.where(inside, offsets, np.sign(offsets) * logged.astype(np.int32))
    return np.clip(bucket + span_size, 0, 2 * span_size - 1).astype(np.int32)


def bucket_rows():
    offsets = np.minimum(np.arange(2 * HALF) - (HALF - 1), HALF - 1)
    far = bucket_values(offsets, SPAN)
    near = bucket_values(-offsets, SPAN)
    return np.stack([near, far]).astype(np.int32)


def mm(a, b):
    return lax.dot_general(a, b, (((1,), (0,)), ((), ())), preferred_element_type=f32)


def mm_t(a, b):
    return lax.dot_general(a, b, (((1,), (1,)), ((), ())), preferred_element_type=f32)


def tmm(a, b):
    return lax.dot_general(a, b, (((0,), (0,)), ((), ())), preferred_element_type=f32)


def iota(shape, dim):
    return lax.broadcasted_iota(jnp.int32, shape, dim)


def loop(count, body):
    def step(index, carry):
        body(index)
        return carry

    lax.fori_loop(0, count, step, 0)


def block(index, size):
    return pl.ds(pl.multiple_of(index * size, size), size)


def mean_row(values):
    return jnp.sum(values, axis=1, keepdims=True) * (1.0 / D)


def whole(ref):
    return ref[...].reshape(-1, ref.shape[-1])


def columns(ref, cols):
    picked = ref[:, :, :, :, cols]
    return picked.reshape(-1, picked.shape[-1])


SCRATCH = dict(
    shift=((L, L), bf16),
    unshift=((L, L), bf16),
    flip=((HALF, HALF), bf16),
    mask=((2, HALF, HALF), f32),
    tok=((L, D), bf16),
    cot=((L, D), bf16),
    pk_near_t=((D, L), bf16),
    pk_far_t=((D, L), bf16),
    pq_far_t=((D, L), bf16),
    emb_near=((L, D), bf16),
    emb_far=((L, D), bf16),
    q=((L, D), bf16),
    k=((L, D), bf16),
    v=((L, D), bf16),
    qt=((D, L), bf16),
    kt=((D, L), bf16),
    k_rev_t=((D, L), bf16),
    g_t=((D, L), bf16),
    v_rev=((L, D), bf16),
    v_rev_t=((D, L), bf16),
    probs=((H, L, HALF), bf16),
    probs_t=((H, L, HALF), bf16),
    ctx=((L, D), bf16),
    attn_pt=((4 * R, D), bf16),
    attn_qt=((4 * R, D), bf16),
    up_pt=((R, FF), bf16),
    up_qt=((R, D), bf16),
    down_pt=((R, D), bf16),
    down_qt=((R, FF), bf16),
    lam_row=((8, 4 * R), f32),
    lam_col=((4 * R, 1), f32),
    u_t=((4 * R, L), f32),
    du_t=((4 * R, L), bf16),
    u_pos_t=((4 * R, L), f32),
    u_up_t=((R, L), f32),
    u_down_t=((R, L), f32),
    xhat1=((L, D), f32),
    rs1=((L, 1), f32),
    hidden=((L, D), f32),
    hid=((L, D), bf16),
    act=((L, FF), bf16),
    slope=((L, FF), bf16),
    branch=((L, D), f32),
    gsum2=((L, D), f32),
    gb5=((L, D), bf16),
    gpk_t=((D, L), bf16),
    gpq_t=((D, L), bf16),
)

GATHERED = dict(
    wqkv=((3, 4, 2, 2, 48, D), bf16),
    wout=((4, 2, 2, 48, D), bf16),
    wup=((4, 2, 2, 48, FF), bf16),
    wdown=((4, 2, 2, 48, FF), bf16),
    embed=((4, 2, 2, 32, D), bf16),
)

ALIASES = dict(
    gpre="slope",
    gsum1="gsum2",
    gb3="gb5",
    gctx="q",
    gq_t="kt",
    gk_t="pk_near_t",
    gv_t="v_rev_t",
    low_out="layer_out",
)

INPUTS = [
    "tokens",
    "cotangent",
    "segments",
    "buckets",
    "attn_bias",
    "up_bias",
    "down_bias",
    "norm_gain",
    "norm_bias",
    "attn_p",
    "attn_q",
    "up_p",
    "up_q",
    "down_p",
    "down_q",
    "lam",
]
SHARDS = [name + "_shard" for name in GATHERED]
IN_HBM = ["tokens", "cotangent"]
OUTPUTS = ["layer_out", "grad_tokens"]
GRADS = dict(
    grad_wide=((2 * R, FF), f32),
    grad_narrow=((2 * R, D), f32),
    grad_fourth=((2 * R, D), f32),
    grad_attn=((6 * R, D), f32),
    grad_lam=((8, 128), f32),
)


class Refs:
    pass


def as_column(row):
    return jnp.transpose(jnp.broadcast_to(row, (128, row.shape[1])))[:, 0:1]


def rank_group(n):
    rank = iota((4 * R, 1), 0)
    return ((rank >= R * n) & (rank < R * (n + 1))).astype(f32)


def prepare_masks(r):
    seg_row = r.segments[...]
    seg_col = as_column(seg_row)
    same = (seg_col == seg_row).astype(f32)
    width = jnp.sum(same, axis=0, keepdims=True)
    place = iota((1, L), 1).astype(f32)
    start = jnp.min(jnp.where(width == float(HALF), place, float(L)), axis=1, keepdims=True)
    row, col = iota((L, L), 0).astype(f32), iota((L, L), 1).astype(f32)
    ahead = row + start
    ahead = jnp.where(ahead >= float(L), ahead - float(L), ahead)
    r.shift[...] = (col == ahead).astype(bf16)
    back = col + start
    back = jnp.where(back >= float(L), back - float(L), back)
    r.unshift[...] = (row == back).astype(bf16)
    r.flip[...] = (iota((HALF, HALF), 0) + iota((HALF, HALF), 1) == HALF - 1).astype(bf16)
    seg_low = jnp.broadcast_to(seg_row.astype(f32), (8, L)).astype(bf16)
    moved_row = mm_t(seg_low, r.shift[...])[0:1, :]
    moved_col = as_column(moved_row)
    for b in range(2):
        rows = slice(HALF * b, HALF * (b + 1))
        r.mask[b] = jnp.where(moved_col[rows, :] == moved_row[:, rows], 0.0, -1e30)


def prepare_factors(r):
    copies = [
        pltpu.make_async_copy(source, target, r.load_sem.at[i])
        for i, (source, target) in enumerate(((r.tokens, r.tok), (r.cotangent, r.cot)))
    ]
    for copy in copies:
        copy.start()
    r.attn_pt[...] = jnp.concatenate([r.attn_p[:, n, :] for n in range(4)], axis=0).astype(bf16)
    r.attn_qt[...] = jnp.concatenate([r.attn_q[:, n, :] for n in range(4)], axis=0).astype(bf16)
    r.up_pt[...] = r.up_p[...].astype(bf16)
    r.up_qt[...] = r.up_q[...].astype(bf16)
    r.down_pt[...] = r.down_p[...].astype(bf16)
    r.down_qt[...] = r.down_q[...].astype(bf16)
    for n in range(4):
        r.lam_row[0:1, R * n : R * (n + 1)] = r.lam[n : n + 1, :]
    r.lam_col[...] = as_column(r.lam_row[0:1, :])
    copies[0].wait()
    r.tok[...] = mm(r.shift[...], r.tok[...]).astype(bf16)
    copies[1].wait()
    r.cot[...] = mm(r.shift[...], r.cot[...]).astype(bf16)


def embed_positions(r):
    column = iota((L, L), 1)
    near_table, far_table = ((as_column(r.buckets[i : i + 1, :]) == column).astype(bf16) for i in range(2))
    r.emb_near[...] = mm(near_table, whole(r.embed)).astype(bf16)
    r.emb_far[...] = mm(far_table, whole(r.embed)).astype(bf16)
    r.u_pos_t[...] = mm_t(r.attn_qt[...], r.emb_far[...])


def project_position(n, near, out, r):
    emb = r.emb_near if near else r.emb_far
    u = mm_t(r.attn_qt[...], emb[...]) if near else r.u_pos_t[...]
    mixed_t = (u * r.lam_col[...] * rank_group(n)).astype(bf16)
    result = (
        mm(emb[...], whole(r.wqkv.at[n]))
        + r.attn_bias[n : n + 1, :].astype(f32)
        + tmm(mixed_t, r.attn_pt[...])
    ).astype(bf16)
    getattr(r, out)[...] = jnp.transpose(result)


def reduce_tokens(r):
    r.u_t[...] = mm_t(r.attn_qt[...], r.tok[...])


def project_token(n, out, r):
    mixed_t = (r.u_t[...] * r.lam_col[...] * rank_group(n)).astype(bf16)
    getattr(r, out)[...] = (
        mm(r.tok[...], whole(r.wqkv.at[n]))
        + r.attn_bias[n : n + 1, :].astype(f32)
        + tmm(mixed_t, r.attn_pt[...])
    ).astype(bf16)


def flip_columns(r, source, target):
    for b in range(2):
        cols = slice(HALF * b, HALF * (b + 1))
        target[:, cols] = mm(source[:, cols], r.flip[...]).astype(bf16)


def arrange_heads(r):
    for b in range(2):
        rows = slice(HALF * b, HALF * (b + 1))
        r.v_rev[rows, :] = mm(r.flip[...], r.v[rows, :]).astype(bf16)
    r.v_rev_t[...] = jnp.transpose(r.v_rev[...])
    r.qt[...] = jnp.transpose(r.q[...])
    r.kt[...] = jnp.transpose(r.k[...])
    flip_columns(r, r.kt, r.k_rev_t)


def head_lanes(a):
    lane = iota((1, 2 * DH), 1)
    return ((lane >= DH) if a else (lane < DH)).astype(bf16)


def attend(r, before=None):
    def pair(p):
        cols = block(p, 2 * DH)
        high = iota((HALF, HALF), 1) + iota((HALF, HALF), 0) >= HALF - 1
        for b in range(2):
            if before is not None:
                before(p, b)
            rows = slice(HALF * b, HALF * (b + 1))
            q, k, v = r.q[rows, cols], r.k[rows, cols], r.v[rows, cols]
            keys = r.kt[cols, rows]
            near_keys, far_queries = r.pk_near_t[cols, :], r.pq_far_t[cols, :]
            probs = []
            for a in range(2):
                lanes = head_lanes(a)
                qa, ka = q * lanes, k * lanes
                content, to, fro = mm(qa, keys), mm(qa, near_keys), mm(ka, far_queries)
                near = jnp.where(high, to[:, :HALF], to[:, HALF:])
                near = pltpu.roll(near, 1, 1, stride=1, stride_axis=0)
                far = jnp.where(high, fro[:, :HALF], fro[:, HALF:])
                far = pltpu.roll(far, 1, 1, stride=1, stride_axis=0)
                scores = (content + near + jnp.transpose(far)) * SCALE + r.mask[b]
                peak = jnp.max(scores, axis=1, keepdims=True)
                terms = jnp.exp(scores - peak)
                total = jnp.sum(terms, axis=1, keepdims=True)
                probs.append((terms * (1.0 / total)).astype(bf16))
            context = mm(probs[0], v * head_lanes(0)) + mm(probs[1], v * head_lanes(1))
            turned = [mm(probs[a], r.flip[...]).astype(bf16) for a in range(2)]
            turned_t = [jnp.transpose(turned[a]) for a in range(2)]
            for a in range(2):
                r.probs[2 * p + a, rows, :] = turned[a]
                r.probs_t[2 * p + a, rows, :] = turned_t[a]
            r.ctx[rows, cols] = context.astype(bf16)

    loop(H // 2, pair)


def out_project(r):
    ctx = r.ctx[...]
    u = mm_t(r.attn_qt[...], ctx)
    r.u_t[3 * R :, :] = u[3 * R :, :]
    mixed_t = (u * r.lam_col[...] * rank_group(3)).astype(bf16)
    r.hidden[...] = (
        mm(ctx, whole(r.wout))
        + r.attn_bias[3:4, :].astype(f32)
        + tmm(mixed_t, r.attn_pt[...])
    )
    gain, bias = r.norm_gain[0:1, :].astype(f32), r.norm_bias[0:1, :].astype(f32)

    def part(i):
        rows = block(i, 128)
        total = r.tok[rows, :].astype(f32) + r.hidden[rows, :]
        centre = total - mean_row(total)
        rs = lax.rsqrt(mean_row(centre * centre) + EPS)
        xhat = centre * rs
        hidden = xhat * gain + bias
        r.xhat1[rows, :] = xhat
        r.rs1[rows, :] = rs
        r.hidden[rows, :] = hidden
        r.hid[rows, :] = hidden.astype(bf16)

    loop(L // 128, part)
    r.u_up_t[...] = mm_t(r.up_qt[...], r.hid[...])


UP_BLOCK = 512


def up_project(r, before=None):
    def part(i):
        if before is not None:
            before(i)
        up_block(r, i)

    loop(FF // UP_BLOCK, part)


def up_block(r, i):
    mixed_t = (r.u_up_t[...] * as_column(r.lam[4:5, :])).astype(bf16)
    cols = block(i, UP_BLOCK)
    pre = (
        mm(r.hid[...], columns(r.wup, cols))
        + r.up_bias[:, cols].astype(f32)
        + tmm(mixed_t, r.up_pt[:, cols])
    )
    phi = 0.5 * (1.0 + lax.erf(pre * np.float32(np.sqrt(0.5))))
    r.act[:, cols] = (pre * phi).astype(bf16)
    bell = jnp.exp(-0.5 * pre * pre) * np.float32(1.0 / np.sqrt(2.0 * np.pi))
    r.slope[:, cols] = (phi + pre * bell).astype(bf16)


def down_reduce(r):
    r.u_down_t[...] = mm_t(r.down_qt[...], r.act[...])


def down_project(r):
    mixed_t = (r.u_down_t[...] * as_column(r.lam[5:6, :])).astype(bf16)
    r.branch[...] = (
        mm_t(r.act[...], whole(r.wdown))
        + r.down_bias[...].astype(f32)
        + tmm(mixed_t, r.down_pt[...])
    )


def norm_two(r):
    gain, bias = r.norm_gain[1:2, :].astype(f32), r.norm_bias[1:2, :].astype(f32)

    def part(i):
        rows = block(i, 128)
        total = r.hidden[rows, :] + r.branch[rows, :]
        centre = total - mean_row(total)
        rs = lax.rsqrt(mean_row(centre * centre) + EPS)
        xhat = centre * rs
        r.low_out[rows, :] = (xhat * gain + bias).astype(bf16)
        e = r.cot[rows, :].astype(f32) * gain
        grad = rs * (e - mean_row(e) - xhat * mean_row(e * xhat))
        r.gsum2[rows, :] = grad
        r.gb5[rows, :] = grad.astype(bf16)

    loop(L // 128, part)


def back_factors(gb, p_t, u_t, lam):
    dmixed = mm_t(p_t, gb)
    return mm((u_t * lam).astype(bf16), gb), (dmixed * lam).astype(bf16), dmixed * u_t


def as_row(column):
    return jnp.transpose(jnp.broadcast_to(column, (column.shape[0], 128)))[0:1, :]


BACK_BLOCK = 1024


def down_back(r):
    gb = r.gb5[...]
    dp, du, dlam = back_factors(gb, r.down_pt[...], r.u_down_t[...], as_column(r.lam[5:6, :]))
    r.grad_narrow[R:, :] = dp
    r.grad_lam[5:6, 0:R] = as_row(jnp.sum(dlam, axis=1, keepdims=True))[:, 0:R]

    def part(i):
        cols = block(i, BACK_BLOCK)
        grad = mm(gb, columns(r.wdown, cols)) + tmm(du, r.down_qt[:, cols])
        r.grad_wide[R:, cols] = mm(du, r.act[:, cols])
        r.gpre[:, cols] = (grad * r.slope[:, cols].astype(f32)).astype(bf16)

    loop(FF // BACK_BLOCK, part)


def up_back(r):
    gb = r.gpre[...]
    dp, du, dlam = back_factors(gb, r.up_pt[...], r.u_up_t[...], as_column(r.lam[4:5, :]))
    r.grad_wide[:R, :] = dp
    r.grad_lam[4:5, 0:R] = as_row(jnp.sum(dlam, axis=1, keepdims=True))[:, 0:R]
    r.grad_narrow[:R, :] = mm(du, r.hid[...])
    r.branch[...] = mm_t(gb, whole(r.wup)) + tmm(du, r.up_qt[...])
    gain = r.norm_gain[0:1, :].astype(f32)

    def part(i):
        rows = block(i, 128)
        e = (r.gsum2[rows, :] + r.branch[rows, :]) * gain
        xhat = r.xhat1[rows, :]
        grad = r.rs1[rows, :] * (e - mean_row(e) - xhat * mean_row(e * xhat))
        r.gsum1[rows, :] = grad
        r.gb3[rows, :] = grad.astype(bf16)

    loop(L // 128, part)


def out_back(r):
    gb = r.gb3[...]
    dp, du, dlam = back_factors(gb, r.attn_pt[...], r.u_t[...], r.lam_col[...] * rank_group(3))
    r.grad_fourth[:R, :] = dp[3 * R :, :]
    r.grad_fourth[R:, :] = mm(du, r.ctx[...])[3 * R :, :]
    r.grad_lam[0:1, 0 : 4 * R] = as_row(jnp.sum(dlam * rank_group(3), axis=1, keepdims=True))
    r.gctx[...] = (mm_t(gb, whole(r.wout)) + tmm(du, r.attn_qt[...])).astype(bf16)
    r.g_t[...] = jnp.transpose(r.gctx[...])


def attend_back(r, before=None):
    def pair(p):
        if before is not None:
            before(p)
        cols = block(p, 2 * DH)
        low = iota((HALF, HALF), 1) >= iota((HALF, HALF), 0)
        zero = jnp.zeros((HALF, HALF), bf16)
        units = [(a, b) for a in range(2) for b in range(2)]
        part = [slice(HALF * b, HALF * (b + 1)) for b in range(2)]
        feats = [block(2 * p + a, DH) for a in range(2)]
        ready, stores = {}, []
        for a, b in units:
            rows, head, lanes = part[b], 2 * p + a, head_lanes(a)
            gprobs = mm(r.gctx[rows, cols] * lanes, r.v_rev_t[cols, rows])
            gprobs_t = mm(r.v_rev[rows, cols] * lanes, r.g_t[cols, rows])
            probs = r.probs[head, rows, :].astype(f32)
            delta = jnp.sum(probs * gprobs, axis=1, keepdims=True)
            gs = (probs * (gprobs - delta)).astype(bf16)
            probs_t = r.probs_t[head, rows, :].astype(f32)
            delta_t = jnp.sum(probs_t * gprobs_t, axis=0, keepdims=True)
            gs_t = (probs_t * (gprobs_t - delta_t)).astype(bf16)
            ready[a, b] = gs, gs_t
        for a in range(2):
            gpk = gpq = None
            for b in range(2):
                rows = part[b]
                gs, gs_t = ready[a, b]
                turn = pltpu.roll(gs, 0, 1, stride=1, stride_axis=0)
                to = jnp.concatenate([jnp.where(low, turn, zero), jnp.where(low, zero, turn)], axis=1)
                turn_t = pltpu.roll(gs_t, 0, 1, stride=1, stride_axis=0)
                fro = jnp.concatenate([jnp.where(low, turn_t, zero), jnp.where(low, zero, turn_t)], axis=1)
                queries, keys = r.qt[feats[a], rows], r.k_rev_t[feats[a], rows]
                gq = mm(keys, gs_t) + mm_t(r.pk_far_t[feats[a], :], to)
                gk = mm(queries, gs) + mm_t(r.pq_far_t[feats[a], :], fro)
                gv = mm(r.g_t[feats[a], rows], r.probs[2 * p + a, rows, :])
                gpk_b, gpq_b = mm(queries, to), mm(keys, fro)
                gpk = gpk_b if gpk is None else gpk + gpk_b
                gpq = gpq_b if gpq is None else gpq + gpq_b
                stores.append((r.gq_t, feats[a], rows, gq * SCALE))
                stores.append((r.gk_t, feats[a], rows, gk * SCALE))
                stores.append((r.gv_t, feats[a], rows, gv))
            stores.append((r.gpk_t, feats[a], slice(None), gpk * SCALE))
            stores.append((r.gpq_t, feats[a], slice(None), gpq * SCALE))
        for ref, feat, rows, value in stores:
            ref[feat, rows] = value.astype(bf16)

    loop(H // 2, pair)


def qkv_factors(r):
    flip_columns(r, r.gk_t, r.gk_t)
    flip_columns(r, r.gv_t, r.gv_t)
    lam = r.lam_col[...]
    u = r.u_t[...]
    dmixed = jnp.zeros((4 * R, L), f32)
    ap = jnp.zeros((4 * R, D), f32)
    for n, g in ((0, r.gq_t), (1, r.gk_t), (2, r.gv_t)):
        gb = g[...]
        dmixed += mm(r.attn_pt[...], gb) * rank_group(n)
        ap += mm_t((u * lam * rank_group(n)).astype(bf16), gb)
    du = (dmixed * lam).astype(bf16)
    r.du_t[...] = du
    aq = mm(du, r.tok[...])
    lam_grad = dmixed * u
    u = r.u_pos_t[...]
    for n, grads in ((0, r.gpq_t), (1, r.gpk_t)):
        gb = grads[...]
        dmixed = mm(r.attn_pt[...], gb) * rank_group(n)
        ap += mm_t((u * lam * rank_group(n)).astype(bf16), gb)
        aq += mm((dmixed * lam).astype(bf16), r.emb_far[...])
        lam_grad += dmixed * u
    r.grad_attn[: 3 * R, :] = ap[: 3 * R, :]
    r.grad_attn[3 * R :, :] = aq[: 3 * R, :]
    r.grad_lam[0:1, 0 : 4 * R] += as_row(jnp.sum(lam_grad, axis=1, keepdims=True))


def qkv_input(r):
    grad_t = tmm(r.attn_qt[...], r.du_t[...])
    for n, g in ((0, r.gq_t), (1, r.gk_t), (2, r.gv_t)):
        grad_t += mm(whole(r.wqkv.at[n]), g[...])
    r.gsum1[...] += jnp.transpose(grad_t)


def finish_layer(r):
    r.layer_out[...] = mm(r.unshift[...], r.low_out[...]).astype(bf16)


def finish_grad(r):
    r.grad_tokens[...] = mm(r.unshift[...], r.gsum1[...].astype(bf16)).astype(bf16)


MESH = pl.DeviceIdType.MESH
SLOTS = 6
ALL = slice(None)
WIDTH = dict(wqkv=384, wout=384, wup=1536, wdown=1536, embed=384)


class Gather:
    def __init__(self, r):
        self.r, self.parts = r, PARTS
        group = lax.axis_index("group")
        self.x = lax.axis_index("inner")
        self.z, self.y, self.c = group // 4, (group // 2) % 2, group % 2

    def device(self, x=None, y=None, z=None, c=None):
        x = self.x if x is None else x
        y = self.y if y is None else y
        z = self.z if z is None else z
        c = self.c if c is None else c
        return ((z * 2 + y) * 2 + c, x)

    def greet(self):
        barrier = pltpu.get_barrier_semaphore()
        partners = [self.device(x=1 - self.x), self.device(y=1 - self.y), self.device(c=1 - self.c)]
        partners += [self.device(z=(self.z + j) % 4) for j in (1, 2, 3)]
        for partner in partners:
            pl.semaphore_signal(barrier, inc=1, device_id=partner, device_id_type=MESH)
        pl.semaphore_wait(barrier, len(partners))

    def region(self, p, z, y, c, x):
        name, lead, start, count, _ = self.parts[p]
        ref = getattr(self.r, name)
        ref = ref if lead is None else ref.at[lead]
        width = WIDTH[name]
        cols = ALL if x is None else pl.ds(pl.multiple_of(x * width, 128), width)
        return ref.at[z, y, c, pl.ds(start, count), cols]

    def shard(self, p):
        name, lead, start, count, _ = self.parts[p]
        ref = getattr(self.r, name + "_shard")
        ref = ref if lead is None else ref.at[lead]
        return ref.at[pl.ds(start, count), :]

    def remote(self, source, target, p, slot, device):
        return pltpu.make_async_remote_copy(
            source,
            target,
            self.r.send_sem.at[p, slot],
            self.r.recv_sem.at[p, slot],
            device_id=device,
            device_id_type=MESH,
        )

    def place_own(self, p):
        target = self.region(p, self.z, self.y, self.c, self.x)
        return pltpu.make_async_copy(self.shard(p), target, self.r.local_sem.at[p])

    def held(self, p, done, c):
        z = ALL if "z" in done else self.z
        y = ALL if "y" in done else self.y
        return self.region(p, z, y, c, None if "x" in done else self.x)

    def outgoing(self, p, k, own=None):
        route = self.parts[p][4]
        region = self.held(p, route[:k], self.c)
        source = region if own is None else own
        if route[k] == "z":
            devices = [self.device(z=(self.z + j) % 4) for j in (1, 2, 3)]
        else:
            devices = [self.device(y=1 - self.y) if route[k] == "y" else self.device(x=1 - self.x)]
        return [self.remote(source, region, p, k, device) for device in devices]

    def arriving(self, p, k, c):
        route = self.parts[p][4]
        done = route[:k]
        z = ALL if "z" in done else self.z
        y = ALL if "y" in done else self.y
        x = None if "x" in done else self.x
        if route[k] == "z":
            return [self.region(p, (self.z + j) % 4, y, c, x) for j in (1, 2, 3)]
        if route[k] == "y":
            return [self.region(p, z, 1 - self.y, c, x)]
        return [self.region(p, z, y, c, 1 - self.x)]

    def amount(self, p, k):
        route = self.parts[p][4]
        if route[k] != "z":
            return self.held(p, route[:k], self.c)
        y = ALL if "y" in route[:k] else self.y
        return self.region(p, pl.ds(0, 3), y, self.c, None if "x" in route[:k] else self.x)

    def sibling(self, p, k, c):
        regions = [self.held(p, self.parts[p][4][:1], c)] if k == 0 else self.arriving(p, k, c)
        device = self.device(c=1 - self.c)
        return [self.remote(ref, ref, p, 3 + k, device) for ref in regions]

    def sibling_amount(self, p, k):
        ref = self.held(p, self.parts[p][4][:1], self.c) if k == 0 else self.amount(p, k)
        return self.remote(ref, ref, p, 3 + k, self.device(c=1 - self.c))

    def start(self, copies):
        for copy in copies:
            copy.start()

    def begin(self, p):
        self.place_own(p).start()
        self.start(self.outgoing(p, 0, self.shard(p)))

    def event(self, p, k):
        self.stage_amount(p, k).wait_recv()
        if k == 0:
            self.place_own(p).wait()
        if k < 2:
            self.start(self.outgoing(p, k + 1))
        self.start(self.sibling(p, k, self.c))

    def stage_amount(self, p, k):
        ref = self.amount(p, k)
        return self.remote(ref, ref, p, k, self.device(c=1 - self.c))

    def ready(self, p):
        for k in range(3):
            self.sibling_amount(p, k).wait_recv()

    def drain(self):
        for p in range(len(self.parts)):
            for k in range(3):
                self.stage_amount(p, k).wait_send()
                self.sibling_amount(p, k).wait_send()


class Exchange:
    def __init__(self, r, comm, name, index):
        self.comm, self.index = comm, index
        self.pack = getattr(r, "pack_" + name)
        self.swap = getattr(r, "swap_" + name)
        self.mine = getattr(r, "mine_" + name)
        self.terms = getattr(r, "terms_" + name)
        self.sums = getattr(r, "sums_" + name)
        self.send_sem, self.recv_sem = r.sum_send, r.sum_recv
        self.chip = comm.z * 2 + comm.y

    def remote(self, source, target, stage, device):
        return pltpu.make_async_remote_copy(
            source,
            target,
            self.send_sem.at[self.index, stage],
            self.recv_sem.at[self.index, stage],
            device_id=device,
            device_id_type=MESH,
        )

    def fill(self, sources):
        count = self.pack.shape[3]
        tile = 0
        for ref, width in sources:
            for row in range(ref.shape[0] // 8):
                for col in range(width // 128):
                    core, chip, slot = tile // (8 * count), tile // count % 8, tile % count
                    for x in range(2):
                        start = (x * width if ref.shape[1] > width else 0) + 128 * col
                        self.pack[x, core, chip, slot] = ref[8 * row : 8 * row + 8, start : start + 128]
                    tile += 1
        while tile < 16 * count:
            core, chip, slot = tile // (8 * count), tile // count % 8, tile % count
            for x in range(2):
                self.pack[x, core, chip, slot] = jnp.zeros((8, 128), f32)
            tile += 1

    def swap_copy(self):
        c = self.comm.c
        return self.remote(self.pack.at[:, 1 - c], self.swap, 0, self.comm.device(c=1 - c))

    def chip_copies(self):
        own = self.comm.x * 8 + self.chip
        for j in range(1, 16):
            index = (own + j) % 16
            x, chip = index // 8, index % 8
            yield self.remote(self.mine.at[x, chip], self.terms.at[own], 1, (chip * 2 + self.comm.c, x))

    def sum_copies(self):
        own = self.chip * 2 + self.comm.c
        slot = self.sums.at[own]
        for j in range(1, 16):
            yield self.remote(slot, slot, 2, ((own + j) % 16, self.comm.x))

    def all_copies(self, stage):
        ref = (self.terms if stage == 1 else self.sums).at[pl.ds(0, 15)]
        return self.remote(ref, ref, stage, self.comm.device(c=1 - self.comm.c))

    def start(self, sources):
        self.fill(sources)
        self.swap_copy().start()

    def spread(self):
        self.swap_copy().wait_recv()
        comm = self.comm
        for x in range(2):
            self.mine[x] = self.pack[x, comm.c] + self.swap[x]
        for copy in self.chip_copies():
            copy.start()
        self.terms[comm.x * 8 + self.chip] = self.mine[comm.x, self.chip]

    def add(self):
        self.all_copies(1).wait_recv()
        total = self.terms[0]
        for index in range(1, 16):
            total = total + self.terms[index]
        self.sums[self.chip * 2 + self.comm.c] = total
        for copy in self.sum_copies():
            copy.start()

    def collect(self):
        self.all_copies(2).wait_recv()

    def drain(self):
        self.swap_copy().wait_send()
        self.all_copies(1).wait_send()
        self.all_copies(2).wait_send()


def exchange_scratch(name, count):
    tiles = (count, 8, 128)
    return {
        "pack_" + name: ((2, 2, 8) + tiles, f32),
        "swap_" + name: ((2, 8) + tiles, f32),
        "mine_" + name: ((2, 8) + tiles, f32),
        "terms_" + name: ((16,) + tiles, f32),
    }


PARTS = (
    ("embed", None, 0, 32, "zxy"),
    ("wqkv", 0, 0, 48, "zyx"),
    ("wqkv", 1, 0, 48, "zxy"),
    ("wqkv", 2, 0, 48, "zyx"),
    ("wout", None, 0, 48, "zyx"),
    ("wup", None, 0, 16, "zxy"),
    ("wup", None, 16, 16, "xzy"),
    ("wup", None, 32, 16, "zyx"),
    ("wdown", None, 0, 16, "zyx"),
    ("wdown", None, 16, 16, "xyz"),
    ("wdown", None, 32, 16, "zxy"),
)
PLAN = (
    ("b", 0),
    ("b", 1),
    ("b", 2),
    ("b", 3),
    ("b", 4),
    ("b", 5),
    ("b", 6),
    ("b", 7),
    ("b", 8),
    ("b", 9),
    ("b", 10),
    ("s", "prep0"),
    ("s", "prep1"),
    (0, 6),
    (0, 9),
    (0, 0),
    (0, 1),
    (1, 9),
    (1, 0),
    (0, 2),
    (1, 1),
    (0, 3),
    (1, 2),
    (0, 4),
    (2, 0),
    ("s", "pos0"),
    (1, 3),
    (0, 5),
    (2, 1),
    ("s", "pos1"),
    (0, 7),
    (2, 2),
    ("s", "pos2"),
    ("s", "pos3"),
    (2, 3),
    (0, 8),
    (1, 4),
    ("s", "qkv0"),
    ("s", "qkv1"),
    ("s", "qkv2"),
    ("s", "qkv3"),
    (1, 5),
    (0, 10),
    (1, 7),
    ("s", "qkv4"),
    ("s", "attend0.0"),
    ("s", "attend0.1"),
    ("s", "attend1.0"),
    (1, 8),
    ("s", "attend1.1"),
    (2, 4),
    ("s", "attend2.0"),
    (1, 6),
    ("s", "attend2.1"),
    ("s", "attend3.0"),
    (1, 10),
    ("s", "attend3.1"),
    (2, 5),
    ("s", "attend4.0"),
    ("s", "attend4.1"),
    ("s", "attend5.0"),
    ("s", "attend5.1"),
    ("s", "out"),
    (2, 7),
    (2, 6),
    ("s", "up0"),
    ("s", "up1"),
    (2, 9),
    ("s", "up2"),
    ("s", "up3"),
    (2, 8),
    ("s", "up4"),
    ("s", "up5"),
    ("s", "down0"),
    (2, 10),
    ("s", "down1"),
)


STEPS = dict(
    prep0=(prepare_masks, ()),
    prep1=(prepare_factors, ()),
    pos0=(embed_positions, ("embed",)),
    pos1=(functools.partial(project_position, 0, False, "pq_far_t"), (("wqkv", 0),)),
    pos2=(functools.partial(project_position, 1, True, "pk_near_t"), (("wqkv", 1),)),
    pos3=(functools.partial(project_position, 1, False, "pk_far_t"), ()),
    qkv0=(reduce_tokens, ()),
    qkv1=(functools.partial(project_token, 0, "q"), ()),
    qkv2=(functools.partial(project_token, 1, "k"), ()),
    qkv3=(functools.partial(project_token, 2, "v"), (("wqkv", 2),)),
    qkv4=(arrange_heads, ()),
    attend=(attend, ()),
    out=(out_project, ("wout",)),
    up=(up_project, ("wup",)),
    down0=(down_reduce, ()),
    down1=(down_project, ("wdown",)),
)
BACKWARD = (
    norm_two,
    down_back,
    up_back,
    out_back,
)


def run_plan(r, comm, plan):
    ready = set()
    waiting = []
    turns = {}
    counts = dict(attend=H, up=FF // UP_BLOCK)

    def moves(items):
        for move in items:
            comm.event(*move)

    def before(*turn):
        for place, items in turns.items():
            if items and place[1:] == turn[1:]:
                pl.when(turn[0] == place[0])(functools.partial(moves, items))

    for kind, arg in plan:
        if kind == "b":
            comm.begin(arg)
            continue
        if kind != "s":
            waiting.append((arg, kind))
            continue
        name = arg.rstrip("0123456789.")
        looped = name in counts
        step, needs = STEPS[name if looped else arg]
        if not looped or not turns:
            moves(waiting)
            waiting = []
            for p, part in enumerate(comm.parts):
                if p not in ready and (part[0] in needs or part[:2] in needs):
                    comm.ready(p)
                    ready.add(p)
        if not looped:
            step(r)
            continue
        turns[tuple(int(c) for c in arg[len(name) :].split("."))] = waiting
        waiting = []
        if len(turns) == counts[name]:
            step(r, before)
            turns = {}
    moves(waiting)


EARLY, LATE = 4, 2
SUMS = dict(sums_early=((16, EARLY, 8, 128), f32), sums_late=((16, LATE, 8, 128), f32))
FUSED_SCRATCH = {
    **SCRATCH,
    **GATHERED,
    **GRADS,
    **exchange_scratch("early", EARLY),
    **exchange_scratch("late", LATE),
}


def layer_kernel(fused, *refs):
    r = Refs()
    if fused:
        names = INPUTS + SHARDS + OUTPUTS + list(SUMS) + list(FUSED_SCRATCH)
        names += ["load_sem", "send_sem", "recv_sem", "local_sem", "sum_send", "sum_recv"]
    else:
        names = INPUTS + list(GATHERED) + OUTPUTS + list(GRADS) + list(SCRATCH) + ["load_sem"]
    for name, ref in zip(names, refs, strict=True):
        setattr(r, name, ref)
    for name, target in ALIASES.items():
        setattr(r, name, getattr(r, target))
    if not fused:
        r.grad_lam[...] = jnp.zeros_like(r.grad_lam)
        for step, _ in STEPS.values():
            step(r)
        for step in BACKWARD + (attend_back, qkv_factors, qkv_input, finish_layer, finish_grad):
            step(r)
        return

    comm = Gather(r)
    comm.greet()
    r.grad_lam[...] = jnp.zeros_like(r.grad_lam)
    run_plan(r, comm, PLAN)
    for step in BACKWARD:
        step(r)
    early = Exchange(r, comm, "early", 0)
    late = Exchange(r, comm, "late", 1)
    early.start(((r.grad_wide, FF // 2), (r.grad_narrow, D // 2), (r.grad_fourth, D // 2)))

    def before(p):
        pl.when(p == 1)(early.spread)
        pl.when(p == 3)(early.add)

    attend_back(r, before)
    qkv_factors(r)
    late.start(((r.grad_attn, D // 2), (r.grad_lam, 128)))
    finish_layer(r)
    late.spread()
    qkv_input(r)
    finish_grad(r)
    comm.drain()
    early.collect()
    early.drain()
    late.add()
    late.collect()
    late.drain()


OUT_SHAPES = dict(layer_out=((L, D), bf16), grad_tokens=((L, D), bf16), **SUMS, **GRADS)


def unpack_kernel(layer_in, grad_in, early, late, layer_out, grad_out, ap, aq, upp, upq, dnp, dnq, glam, *parts):
    layer_out[...] = layer_in[...]
    grad_out[...] = grad_in[...]
    wide, narrow, fourth, attn = parts
    for sums, refs in ((early, (wide, narrow, fourth)), (late, (attn,))):
        count = sums.shape[1]
        tile = 0
        for ref in refs:
            for row in range(ref.shape[0] // 8):
                for col in range(ref.shape[1] // 128):
                    core, chip, slot = tile // (8 * count), tile // count % 8, tile % count
                    ref[8 * row : 8 * row + 8, 128 * col : 128 * col + 128] = sums[chip * 2 + core, slot]
                    tile += 1
    core, chip, slot = tile // (8 * count), tile // count % 8, tile % count
    lam = sums[chip * 2 + core, slot]
    for n in range(4):
        glam[n : n + 1, :] = lam[0:1, R * n : R * (n + 1)]
    glam[4:6, :] = lam[4:6, 0:R]
    upp[...] = wide[:R, :]
    dnq[...] = wide[R:, :]
    upq[...] = narrow[:R, :]
    dnp[...] = narrow[R:, :]
    for n in range(3):
        ap[:, n, :] = attn[R * n : R * (n + 1), :]
        aq[:, n, :] = attn[3 * R + R * n : 3 * R + R * (n + 1), :]
    ap[:, 3, :] = fourth[:R, :]
    aq[:, 3, :] = fourth[R:, :]


def unpack_call(layer_out, grad_tokens, early, late):
    half = D // 2
    vmem = pl.BlockSpec(memory_space=pltpu.VMEM)
    shapes = [
        ((L, D), bf16),
        ((L, D), bf16),
        ((R, 4, half), f32),
        ((R, 4, half), f32),
        ((R, FF // 2), f32),
        ((R, half), f32),
        ((R, half), f32),
        ((R, FF // 2), f32),
        ((6, R), f32),
    ]
    return pl.pallas_call(
        unpack_kernel,
        out_shape=[jax.ShapeDtypeStruct(*shape) for shape in shapes],
        in_specs=[vmem] * 4,
        out_specs=[vmem] * len(shapes),
        scratch_shapes=[
            pltpu.VMEM((2 * R, FF // 2), f32),
            pltpu.VMEM((2 * R, half), f32),
            pltpu.VMEM((2 * R, half), f32),
            pltpu.VMEM((6 * R, half), f32),
        ],
    )(layer_out, grad_tokens, early, late)


def layer_call(args, weights, fused):
    vmem = pl.BlockSpec(memory_space=pltpu.VMEM)
    hbm = pl.BlockSpec(memory_space=pl.ANY)
    load_sem = pltpu.SemaphoreType.DMA((2,))
    if fused:
        outputs = OUTPUTS + list(SUMS)
        scratch = [pltpu.VMEM(*spec) for spec in FUSED_SCRATCH.values()] + [
            load_sem,
            pltpu.SemaphoreType.DMA((len(PARTS), SLOTS)),
            pltpu.SemaphoreType.DMA((len(PARTS), SLOTS)),
            pltpu.SemaphoreType.DMA((len(PARTS),)),
            pltpu.SemaphoreType.DMA((2, 3)),
            pltpu.SemaphoreType.DMA((2, 3)),
        ]
        extra = dict(collective_id=0, has_side_effects=True)
    else:
        outputs = OUTPUTS + list(GRADS)
        scratch = [pltpu.VMEM(*spec) for spec in SCRATCH.values()] + [load_sem]
        weights = [w.reshape(GATHERED[name][0]) for name, w in zip(GATHERED, weights)]
        extra = {}
    return pl.pallas_call(
        functools.partial(layer_kernel, fused),
        out_shape=[jax.ShapeDtypeStruct(*OUT_SHAPES[name]) for name in outputs],
        in_specs=[hbm if name in IN_HBM else vmem for name in INPUTS]
        + [hbm if fused else vmem] * len(weights),
        out_specs=[vmem] * len(outputs),
        scratch_shapes=scratch,
        compiler_params=pltpu.CompilerParams(vmem_limit_bytes=63 * 2**20, **extra),
    )(*args, *weights)


def gather_plain(w_qkv, w_out, w_up, down_t, rel_embed):
    parts = []
    for shard, rows, cols in (
        (w_qkv, 1, 2),
        (w_out, 0, 1),
        (w_up, 0, 1),
        (down_t, 0, 1),
        (rel_embed, 0, 1),
    ):
        part = lax.all_gather(shard, "inner", axis=cols, tiled=True)
        parts.append(lax.all_gather(part, "group", axis=rows, tiled=True))
    return parts


def reduce_plain(grads):
    shared = [
        lax.psum(lax.psum_scatter(g, "inner", scatter_dimension=1, tiled=True), "group")
        for g in grads[:-1]
    ]
    return shared, lax.psum(grads[-1], ("group", "inner"))


def on_device(
    tokens,
    cotangent,
    segments,
    w_qkv,
    w_out,
    w_up,
    w_down,
    rel_embed,
    attn_bias,
    up_bias,
    down_bias,
    norm_gain,
    norm_bias,
    attn_p,
    attn_q,
    up_p,
    up_q,
    down_p,
    down_q,
    lam,
):
    fused = (lax.axis_size("group"), lax.axis_size("inner")) == (16, 2)
    down_t = jnp.transpose(w_down)
    weights = (w_qkv, w_out, w_up, down_t, rel_embed)
    if not fused:
        weights = gather_plain(*weights)
    args = (
        tokens,
        cotangent,
        segments,
        jnp.asarray(bucket_rows()),
        attn_bias,
        up_bias[None],
        down_bias[None],
        norm_gain,
        norm_bias,
        jnp.transpose(attn_p, (2, 1, 0)),
        jnp.transpose(attn_q, (2, 1, 0)),
        up_p.T,
        up_q.T,
        down_p.T,
        down_q.T,
        lam,
    )
    layer_out, grad_tokens, *sums = layer_call(args, weights, fused)
    if fused:
        layer_out, grad_tokens, ap, aq, upp, upq, dnp, dnq, grad_lam = unpack_call(
            layer_out, grad_tokens, *sums
        )
    else:
        (wide, narrow, fourth, attn), lam_sums = reduce_plain(sums)
        by_rank = [attn[R * n : R * (n + 1)] for n in range(6)]
        ap = jnp.stack(by_rank[:3] + [fourth[:R]], axis=1)
        aq = jnp.stack(by_rank[3:] + [fourth[R:]], axis=1)
        upp, dnq, upq, dnp = wide[:R], wide[R:], narrow[:R], narrow[R:]
        grad_lam = jnp.concatenate([lam_sums[0, : 4 * R].reshape(4, R), lam_sums[4:6, :R]], axis=0)
    return (
        layer_out,
        grad_tokens,
        jnp.transpose(ap, (2, 1, 0)),
        jnp.transpose(aq, (2, 1, 0)),
        upp.T,
        upq.T,
        dnp.T,
        dnq.T,
        grad_lam,
    )


def solution(mesh):
    rows = P(("group", "inner"), None)
    return jax.shard_map(
        on_device,
        mesh=mesh,
        in_specs=(
            rows,
            rows,
            rows,
            P(None, "group", "inner"),
            P("group", "inner"),
            P("group", "inner"),
            P("inner", "group"),
            P("group", "inner"),
        )
        + (P(),) * 12,
        out_specs=(
            rows,
            rows,
            P("inner", None, None),
            P("inner", None, None),
            P("inner", None),
            P("inner", None),
            P("inner", None),
            P("inner", None),
            P(),
        ),
        check_vma=False,
    )
```

```python
import functools

import jax
import jax.numpy as jnp
import numpy as np
from jax import lax
from jax.experimental import pallas as pl
from jax.experimental.pallas import tpu as pltpu
from jax.sharding import PartitionSpec as P

D = 768
H = 12
DH = 64
FF = 3072
SPAN = 256
L = 512
R = 12
HALF = L // 2
SCALE = (3.0 * DH) ** (-0.5)
EPS = 1e-07

bf16 = jnp.bfloat16
f32 = jnp.float32


def bucket_values(offsets, span_size):
    middle = span_size // 2
    magnitude = np.abs(offsets)
    inside = magnitude <= middle
    clipped = np.maximum(magnitude, middle) * 1.0
    logged = (
        np.ceil(np.log(clipped / middle) / np.log((2 * span_size - 1) / middle) * (middle - 1))
        + middle
    )
    bucket = np.where(inside, offsets, np.sign(offsets) * logged.astype(np.int32))
    return np.clip(bucket + span_size, 0, 2 * span_size - 1).astype(np.int32)


def bucket_rows():
    offsets = np.minimum(np.arange(2 * HALF) - (HALF - 1), HALF - 1)
    far = bucket_values(offsets, SPAN)
    near = bucket_values(-offsets, SPAN)
    return np.stack([near, far]).astype(np.int32)


def mm(a, b):
    return lax.dot_general(a, b, (((1,), (0,)), ((), ())), preferred_element_type=f32)


def mm_t(a, b):
    return lax.dot_general(a, b, (((1,), (1,)), ((), ())), preferred_element_type=f32)


def tmm(a, b):
    return lax.dot_general(a, b, (((0,), (0,)), ((), ())), preferred_element_type=f32)


def iota(shape, dim):
    return lax.broadcasted_iota(jnp.int32, shape, dim)


def loop(count, body):
    def step(index, carry):
        body(index)
        return carry

    lax.fori_loop(0, count, step, 0)


def block(index, size):
    return pl.ds(pl.multiple_of(index * size, size), size)


def mean_row(values):
    return jnp.sum(values, axis=1, keepdims=True) * (1.0 / D)


def flat(block):
    return block.reshape(-1, block.shape[-1])


def whole(ref):
    return jnp.concatenate([flat(ref[x]) for x in range(2)], axis=1)


THIRD = FF // 6


def whole_wide(ref):
    return jnp.concatenate([flat(ref[t, x]) for x in range(2) for t in range(3)], axis=1)


def third(t, x):
    return pl.ds(pl.multiple_of((3 * x + t) * THIRD, THIRD), THIRD)


SCRATCH = dict(
    shift=((L, L), bf16),
    unshift=((L, L), bf16),
    flip=((HALF, HALF), bf16),
    mask=((2, HALF, HALF), f32),
    tok=((L, D), bf16),
    cot=((L, D), bf16),
    pk_near_t=((D, L), bf16),
    pk_far_t=((D, L), bf16),
    pq_far_t=((D, L), bf16),
    emb_near=((L, D), bf16),
    emb_far=((L, D), bf16),
    q=((L, D), bf16),
    k=((L, D), bf16),
    v=((L, D), bf16),
    qt=((D, L), bf16),
    kt=((D, L), bf16),
    k_rev_t=((D, L), bf16),
    g_t=((D, L), bf16),
    v_rev=((L, D), bf16),
    v_rev_t=((D, L), bf16),
    probs=((H, L, HALF), bf16),
    probs_t=((H, L, HALF), bf16),
    ctx=((L, D), bf16),
    attn_pt=((4 * R, D), bf16),
    attn_qt=((4 * R, D), bf16),
    up_pt=((R, FF), bf16),
    up_qt=((R, D), bf16),
    down_pt=((R, D), bf16),
    down_qt=((R, FF), bf16),
    lam_row=((8, 4 * R), f32),
    lam_col=((4 * R, 1), f32),
    up_row=((1, FF), f32),
    down_row=((1, D), f32),
    u_t=((4 * R, L), f32),
    du_t=((4 * R, L), bf16),
    u_pos_t=((4 * R, L), f32),
    u_up_t=((R, L), f32),
    u_down_t=((R, L), f32),
    xhat1=((L, D), f32),
    rs1=((L, 1), f32),
    hidden=((L, D), f32),
    hid=((L, D), bf16),
    act=((L, FF), bf16),
    slope=((L, FF), bf16),
    branch=((L, D), f32),
    gsum2=((L, D), f32),
    gb5=((L, D), bf16),
    gpk_t=((D, L), bf16),
    gpq_t=((D, L), bf16),
)

GATHERED = dict(
    wqkv=((3, 2, 4, 2, 2, 48, D // 2), bf16),
    wout=((2, 4, 2, 2, 48, D // 2), bf16),
    wup=((3, 2, 4, 2, 2, 48, THIRD), bf16),
    wdown=((3, 2, 4, 2, 2, 48, THIRD), bf16),
    embed=((2, 4, 2, 2, 32, D // 2), bf16),
)

ALIASES = dict(
    gpre="slope",
    gsum1="gsum2",
    gb3="gb5",
    gctx="q",
    gq_t="kt",
    gk_t="pk_near_t",
    gv_t="v_rev_t",
    low_out="layer_out",
)

INPUTS = [
    "tokens",
    "cotangent",
    "segments",
    "buckets",
    "attn_bias",
    "up_bias",
    "down_bias",
    "norm_gain",
    "norm_bias",
    "attn_p",
    "attn_q",
    "up_p",
    "up_q",
    "down_p",
    "down_q",
    "lam",
]
SHARDS = [name + "_shard" for name in GATHERED]
IN_HBM = ["tokens", "cotangent"]
OUTPUTS = ["layer_out", "grad_tokens"]
GRADS = dict(
    grad_wide=((2 * R, FF), f32),
    grad_narrow=((2 * R, D), f32),
    grad_fourth=((2 * R, D), f32),
    grad_attn=((6 * R, D), f32),
    grad_lam=((8, 128), f32),
)


class Refs:
    pass


def as_column(row):
    return jnp.transpose(jnp.broadcast_to(row, (128, row.shape[1])))[:, 0:1]


def rank_group(n):
    rank = iota((4 * R, 1), 0)
    return ((rank >= R * n) & (rank < R * (n + 1))).astype(f32)


def prepare_masks(r):
    seg_row = r.segments[...]
    seg_col = as_column(seg_row)
    same = (seg_col == seg_row).astype(f32)
    width = jnp.sum(same, axis=0, keepdims=True)
    place = iota((1, L), 1).astype(f32)
    start = jnp.min(jnp.where(width == float(HALF), place, float(L)), axis=1, keepdims=True)
    row, col = iota((L, L), 0).astype(f32), iota((L, L), 1).astype(f32)
    ahead = row + start
    ahead = jnp.where(ahead >= float(L), ahead - float(L), ahead)
    r.shift[...] = (col == ahead).astype(bf16)
    back = col + start
    back = jnp.where(back >= float(L), back - float(L), back)
    r.unshift[...] = (row == back).astype(bf16)
    r.flip[...] = (iota((HALF, HALF), 0) + iota((HALF, HALF), 1) == HALF - 1).astype(bf16)
    seg_low = jnp.broadcast_to(seg_row.astype(f32), (8, L)).astype(bf16)
    moved_row = mm_t(seg_low, r.shift[...])[0:1, :]
    moved_col = as_column(moved_row)
    for b in range(2):
        rows = slice(HALF * b, HALF * (b + 1))
        r.mask[b] = jnp.where(moved_col[rows, :] == moved_row[:, rows], 0.0, -1e30)


def prepare_factors(r):
    copies = [
        pltpu.make_async_copy(source, target, r.load_sem.at[i])
        for i, (source, target) in enumerate(((r.tokens, r.tok), (r.cotangent, r.cot)))
    ]
    for copy in copies:
        copy.start()
    r.attn_pt[...] = jnp.concatenate([r.attn_p[:, n, :] for n in range(4)], axis=0).astype(bf16)
    r.attn_qt[...] = jnp.concatenate([r.attn_q[:, n, :] for n in range(4)], axis=0).astype(bf16)
    r.up_pt[...] = r.up_p[...].astype(bf16)
    r.up_qt[...] = r.up_q[...].astype(bf16)
    r.down_pt[...] = r.down_p[...].astype(bf16)
    r.down_qt[...] = r.down_q[...].astype(bf16)
    for n in range(4):
        r.lam_row[0:1, R * n : R * (n + 1)] = r.lam[n : n + 1, :]
    r.lam_col[...] = as_column(r.lam_row[0:1, :])
    r.up_row[...] = r.up_bias[...].astype(f32).reshape(1, FF)
    r.down_row[...] = r.down_bias[...].astype(f32).reshape(1, D)
    copies[0].wait()
    r.tok[...] = mm(r.shift[...], r.tok[...]).astype(bf16)
    copies[1].wait()
    r.cot[...] = mm(r.shift[...], r.cot[...]).astype(bf16)


def embed_positions(r):
    column = iota((L, L), 1)
    near_table, far_table = ((as_column(r.buckets[i : i + 1, :]) == column).astype(bf16) for i in range(2))
    r.emb_near[...] = mm(near_table, whole(r.embed)).astype(bf16)
    r.emb_far[...] = mm(far_table, whole(r.embed)).astype(bf16)
    r.u_pos_t[...] = mm_t(r.attn_qt[...], r.emb_far[...])


def project_position(n, near, out, r):
    emb = r.emb_near if near else r.emb_far
    u = mm_t(r.attn_qt[...], emb[...]) if near else r.u_pos_t[...]
    mixed_t = (u * r.lam_col[...] * rank_group(n)).astype(bf16)
    result = (
        mm(emb[...], whole(r.wqkv.at[n]))
        + r.attn_bias[n : n + 1, :].astype(f32)
        + tmm(mixed_t, r.attn_pt[...])
    ).astype(bf16)
    getattr(r, out)[...] = jnp.transpose(result)


def reduce_tokens(r):
    r.u_t[...] = mm_t(r.attn_qt[...], r.tok[...])


def project_token(n, out, r):
    mixed_t = (r.u_t[...] * r.lam_col[...] * rank_group(n)).astype(bf16)
    getattr(r, out)[...] = (
        mm(r.tok[...], whole(r.wqkv.at[n]))
        + r.attn_bias[n : n + 1, :].astype(f32)
        + tmm(mixed_t, r.attn_pt[...])
    ).astype(bf16)


def flip_columns(r, source, target):
    for b in range(2):
        cols = slice(HALF * b, HALF * (b + 1))
        target[:, cols] = mm(source[:, cols], r.flip[...]).astype(bf16)


def arrange_heads(r):
    for b in range(2):
        rows = slice(HALF * b, HALF * (b + 1))
        r.v_rev[rows, :] = mm(r.flip[...], r.v[rows, :]).astype(bf16)
    r.v_rev_t[...] = jnp.transpose(r.v_rev[...])
    r.qt[...] = jnp.transpose(r.q[...])
    r.kt[...] = jnp.transpose(r.k[...])
    flip_columns(r, r.kt, r.k_rev_t)


def head_lanes(a):
    lane = iota((1, 2 * DH), 1)
    return ((lane >= DH) if a else (lane < DH)).astype(bf16)


def attend(r, before=None):
    def pair(p):
        cols = block(p, 2 * DH)
        high = iota((HALF, HALF), 1) + iota((HALF, HALF), 0) >= HALF - 1
        for b in range(2):
            if before is not None:
                before(p, b)
            rows = slice(HALF * b, HALF * (b + 1))
            q, k, v = r.q[rows, cols], r.k[rows, cols], r.v[rows, cols]
            keys = r.kt[cols, rows]
            near_keys, far_queries = r.pk_near_t[cols, :], r.pq_far_t[cols, :]
            probs = []
            for a in range(2):
                lanes = head_lanes(a)
                qa, ka = q * lanes, k * lanes
                content, to, fro = mm(qa, keys), mm(qa, near_keys), mm(ka, far_queries)
                near = jnp.where(high, to[:, :HALF], to[:, HALF:])
                near = pltpu.roll(near, 1, 1, stride=1, stride_axis=0)
                far = jnp.where(high, fro[:, :HALF], fro[:, HALF:])
                far = pltpu.roll(far, 1, 1, stride=1, stride_axis=0)
                scores = (content + near + jnp.transpose(far)) * SCALE + r.mask[b]
                peak = jnp.max(scores, axis=1, keepdims=True)
                terms = jnp.exp(scores - peak)
                total = jnp.sum(terms, axis=1, keepdims=True)
                probs.append((terms * (1.0 / total)).astype(bf16))
            context = mm(probs[0], v * head_lanes(0)) + mm(probs[1], v * head_lanes(1))
            turned = [mm(probs[a], r.flip[...]).astype(bf16) for a in range(2)]
            turned_t = [jnp.transpose(turned[a]) for a in range(2)]
            for a in range(2):
                r.probs[2 * p + a, rows, :] = turned[a]
                r.probs_t[2 * p + a, rows, :] = turned_t[a]
            r.ctx[rows, cols] = context.astype(bf16)

    loop(H // 2, pair)


def out_project(r):
    ctx = r.ctx[...]
    u = mm_t(r.attn_qt[...], ctx)
    r.u_t[3 * R :, :] = u[3 * R :, :]
    mixed_t = (u * r.lam_col[...] * rank_group(3)).astype(bf16)
    r.hidden[...] = (
        mm(ctx, whole(r.wout))
        + r.attn_bias[3:4, :].astype(f32)
        + tmm(mixed_t, r.attn_pt[...])
    )
    gain, bias = r.norm_gain[0:1, :].astype(f32), r.norm_bias[0:1, :].astype(f32)

    def part(i):
        rows = block(i, 128)
        total = r.tok[rows, :].astype(f32) + r.hidden[rows, :]
        centre = total - mean_row(total)
        rs = lax.rsqrt(mean_row(centre * centre) + EPS)
        xhat = centre * rs
        hidden = xhat * gain + bias
        r.xhat1[rows, :] = xhat
        r.rs1[rows, :] = rs
        r.hidden[rows, :] = hidden
        r.hid[rows, :] = hidden.astype(bf16)

    loop(L // 128, part)
    r.u_up_t[...] = mm_t(r.up_qt[...], r.hid[...])


def up_project(r, before=None):
    def part(i):
        if before is not None:
            before(i)
        up_block(r, i // 2, i % 2)

    loop(6, part)


def up_block(r, t, x):
    cols = third(t, x)
    mixed_t = (r.u_up_t[...] * as_column(r.lam[4:5, :])).astype(bf16)
    pre = (
        mm(r.hid[...], flat(r.wup[t, x]))
        + r.up_row[:, cols]
        + tmm(mixed_t, r.up_pt[:, cols])
    )
    phi = 0.5 * (1.0 + lax.erf(pre * np.float32(np.sqrt(0.5))))
    r.act[:, cols] = (pre * phi).astype(bf16)
    bell = jnp.exp(-0.5 * pre * pre) * np.float32(1.0 / np.sqrt(2.0 * np.pi))
    r.slope[:, cols] = (phi + pre * bell).astype(bf16)


def down_reduce(r):
    r.u_down_t[...] = mm_t(r.down_qt[...], r.act[...])
    mixed_t = (r.u_down_t[...] * as_column(r.lam[5:6, :])).astype(bf16)
    r.branch[...] = r.down_row[...] + tmm(mixed_t, r.down_pt[...])


def down_third(t, r):
    act = jnp.concatenate([r.act[:, third(t, x)] for x in range(2)], axis=1)
    weight = jnp.concatenate([flat(r.wdown[t, x]) for x in range(2)], axis=1)
    r.branch[...] += mm_t(act, weight)


def norm_two(r):
    gain, bias = r.norm_gain[1:2, :].astype(f32), r.norm_bias[1:2, :].astype(f32)

    def part(i):
        rows = block(i, 128)
        total = r.hidden[rows, :] + r.branch[rows, :]
        centre = total - mean_row(total)
        rs = lax.rsqrt(mean_row(centre * centre) + EPS)
        xhat = centre * rs
        r.low_out[rows, :] = (xhat * gain + bias).astype(bf16)
        e = r.cot[rows, :].astype(f32) * gain
        grad = rs * (e - mean_row(e) - xhat * mean_row(e * xhat))
        r.gsum2[rows, :] = grad
        r.gb5[rows, :] = grad.astype(bf16)

    loop(L // 128, part)


def back_factors(gb, p_t, u_t, lam):
    dmixed = mm_t(p_t, gb)
    return mm((u_t * lam).astype(bf16), gb), (dmixed * lam).astype(bf16), dmixed * u_t


def as_row(column):
    return jnp.transpose(jnp.broadcast_to(column, (column.shape[0], 128)))[0:1, :]


def down_back(r):
    gb = r.gb5[...]
    dp, du, dlam = back_factors(gb, r.down_pt[...], r.u_down_t[...], as_column(r.lam[5:6, :]))
    r.grad_narrow[R:, :] = dp
    r.grad_lam[5:6, 0:R] = as_row(jnp.sum(dlam, axis=1, keepdims=True))[:, 0:R]

    def part(t):
        for x in range(2):
            cols = third(t, x)
            grad = mm(gb, flat(r.wdown[t, x])) + tmm(du, r.down_qt[:, cols])
            r.grad_wide[R:, cols] = mm(du, r.act[:, cols])
            r.gpre[:, cols] = (grad * r.slope[:, cols].astype(f32)).astype(bf16)

    loop(3, part)


def up_back(r):
    gb = r.gpre[...]
    dp, du, dlam = back_factors(gb, r.up_pt[...], r.u_up_t[...], as_column(r.lam[4:5, :]))
    r.grad_wide[:R, :] = dp
    r.grad_lam[4:5, 0:R] = as_row(jnp.sum(dlam, axis=1, keepdims=True))[:, 0:R]
    r.grad_narrow[:R, :] = mm(du, r.hid[...])
    r.branch[...] = mm_t(gb, whole_wide(r.wup)) + tmm(du, r.up_qt[...])
    gain = r.norm_gain[0:1, :].astype(f32)

    def part(i):
        rows = block(i, 128)
        e = (r.gsum2[rows, :] + r.branch[rows, :]) * gain
        xhat = r.xhat1[rows, :]
        grad = r.rs1[rows, :] * (e - mean_row(e) - xhat * mean_row(e * xhat))
        r.gsum1[rows, :] = grad
        r.gb3[rows, :] = grad.astype(bf16)

    loop(L // 128, part)


def out_back(r):
    gb = r.gb3[...]
    dp, du, dlam = back_factors(gb, r.attn_pt[...], r.u_t[...], r.lam_col[...] * rank_group(3))
    r.grad_fourth[:R, :] = dp[3 * R :, :]
    r.grad_fourth[R:, :] = mm(du, r.ctx[...])[3 * R :, :]
    r.grad_lam[0:1, 0 : 4 * R] = as_row(jnp.sum(dlam * rank_group(3), axis=1, keepdims=True))
    r.gctx[...] = (mm_t(gb, whole(r.wout)) + tmm(du, r.attn_qt[...])).astype(bf16)
    r.g_t[...] = jnp.transpose(r.gctx[...])


def attend_back(r, before=None):
    def pair(p):
        if before is not None:
            before(p)
        cols = block(p, 2 * DH)
        low = iota((HALF, HALF), 1) >= iota((HALF, HALF), 0)
        zero = jnp.zeros((HALF, HALF), bf16)
        units = [(a, b) for a in range(2) for b in range(2)]
        part = [slice(HALF * b, HALF * (b + 1)) for b in range(2)]
        feats = [block(2 * p + a, DH) for a in range(2)]
        ready, stores = {}, []
        for a, b in units:
            rows, head, lanes = part[b], 2 * p + a, head_lanes(a)
            gprobs = mm(r.gctx[rows, cols] * lanes, r.v_rev_t[cols, rows])
            gprobs_t = mm(r.v_rev[rows, cols] * lanes, r.g_t[cols, rows])
            probs = r.probs[head, rows, :].astype(f32)
            delta = jnp.sum(probs * gprobs, axis=1, keepdims=True)
            gs = (probs * (gprobs - delta)).astype(bf16)
            probs_t = r.probs_t[head, rows, :].astype(f32)
            delta_t = jnp.sum(probs_t * gprobs_t, axis=0, keepdims=True)
            gs_t = (probs_t * (gprobs_t - delta_t)).astype(bf16)
            ready[a, b] = gs, gs_t
        for a in range(2):
            gpk = gpq = None
            for b in range(2):
                rows = part[b]
                gs, gs_t = ready[a, b]
                turn = pltpu.roll(gs, 0, 1, stride=1, stride_axis=0)
                to = jnp.concatenate([jnp.where(low, turn, zero), jnp.where(low, zero, turn)], axis=1)
                turn_t = pltpu.roll(gs_t, 0, 1, stride=1, stride_axis=0)
                fro = jnp.concatenate([jnp.where(low, turn_t, zero), jnp.where(low, zero, turn_t)], axis=1)
                queries, keys = r.qt[feats[a], rows], r.k_rev_t[feats[a], rows]
                gq = mm(keys, gs_t) + mm_t(r.pk_far_t[feats[a], :], to)
                gk = mm(queries, gs) + mm_t(r.pq_far_t[feats[a], :], fro)
                gv = mm(r.g_t[feats[a], rows], r.probs[2 * p + a, rows, :])
                gpk_b, gpq_b = mm(queries, to), mm(keys, fro)
                gpk = gpk_b if gpk is None else gpk + gpk_b
                gpq = gpq_b if gpq is None else gpq + gpq_b
                stores.append((r.gq_t, feats[a], rows, gq * SCALE))
                stores.append((r.gk_t, feats[a], rows, gk * SCALE))
                stores.append((r.gv_t, feats[a], rows, gv))
            stores.append((r.gpk_t, feats[a], slice(None), gpk * SCALE))
            stores.append((r.gpq_t, feats[a], slice(None), gpq * SCALE))
        for ref, feat, rows, value in stores:
            ref[feat, rows] = value.astype(bf16)

    loop(H // 2, pair)


def qkv_factors(r):
    flip_columns(r, r.gk_t, r.gk_t)
    flip_columns(r, r.gv_t, r.gv_t)
    lam = r.lam_col[...]
    u = r.u_t[...]
    dmixed = jnp.zeros((4 * R, L), f32)
    ap = jnp.zeros((4 * R, D), f32)
    for n, g in ((0, r.gq_t), (1, r.gk_t), (2, r.gv_t)):
        gb = g[...]
        dmixed += mm(r.attn_pt[...], gb) * rank_group(n)
        ap += mm_t((u * lam * rank_group(n)).astype(bf16), gb)
    du = (dmixed * lam).astype(bf16)
    r.du_t[...] = du
    aq = mm(du, r.tok[...])
    lam_grad = dmixed * u
    u = r.u_pos_t[...]
    for n, grads in ((0, r.gpq_t), (1, r.gpk_t)):
        gb = grads[...]
        dmixed = mm(r.attn_pt[...], gb) * rank_group(n)
        ap += mm_t((u * lam * rank_group(n)).astype(bf16), gb)
        aq += mm((dmixed * lam).astype(bf16), r.emb_far[...])
        lam_grad += dmixed * u
    r.grad_attn[: 3 * R, :] = ap[: 3 * R, :]
    r.grad_attn[3 * R :, :] = aq[: 3 * R, :]
    r.grad_lam[0:1, 0 : 4 * R] += as_row(jnp.sum(lam_grad, axis=1, keepdims=True))


def qkv_input(r):
    grad_t = tmm(r.attn_qt[...], r.du_t[...])
    for n, g in ((0, r.gq_t), (1, r.gk_t), (2, r.gv_t)):
        grad_t += mm(whole(r.wqkv.at[n]), g[...])
    r.gsum1[...] += jnp.transpose(grad_t)


def finish_layer(r):
    r.layer_out[...] = mm(r.unshift[...], r.low_out[...]).astype(bf16)


def finish_grad(r):
    r.grad_tokens[...] = mm(r.unshift[...], r.gsum1[...].astype(bf16)).astype(bf16)


MESH = pl.DeviceIdType.MESH
SLOTS = 6
ALL = slice(None)


class Gather:
    def __init__(self, r):
        self.r, self.parts = r, PARTS
        group = lax.axis_index("group")
        self.x = lax.axis_index("inner")
        self.z, self.y, self.c = group // 4, (group // 2) % 2, group % 2

    def device(self, x=None, y=None, z=None, c=None):
        x = self.x if x is None else x
        y = self.y if y is None else y
        z = self.z if z is None else z
        c = self.c if c is None else c
        return ((z * 2 + y) * 2 + c, x)

    def greet(self):
        barrier = pltpu.get_barrier_semaphore()
        partners = [self.device(x=1 - self.x), self.device(y=1 - self.y), self.device(c=1 - self.c)]
        partners += [self.device(z=(self.z + j) % 4) for j in (1, 2, 3)]
        for partner in partners:
            pl.semaphore_signal(barrier, inc=1, device_id=partner, device_id_type=MESH)
        pl.semaphore_wait(barrier, len(partners))

    def region(self, p, z, y, c, x):
        name, lead, _ = self.parts[p]
        ref = getattr(self.r, name)
        ref = ref if lead is None else ref.at[lead]
        return ref.at[ALL if x is None else x, z, y, c]

    def shard(self, p):
        name, lead, _ = self.parts[p]
        ref = getattr(self.r, name + "_shard")
        if lead is None:
            return ref
        return ref.at[lead] if name == "wqkv" else ref.at[:, pl.ds(lead * THIRD, THIRD)]

    def remote(self, source, target, p, slot, device):
        return pltpu.make_async_remote_copy(
            source,
            target,
            self.r.send_sem.at[p, slot],
            self.r.recv_sem.at[p, slot],
            device_id=device,
            device_id_type=MESH,
        )

    def place_own(self, p):
        target = self.region(p, self.z, self.y, self.c, self.x)
        return pltpu.make_async_copy(self.shard(p), target, self.r.local_sem.at[p])

    def held(self, p, done, c):
        z = ALL if "z" in done else self.z
        y = ALL if "y" in done else self.y
        return self.region(p, z, y, c, None if "x" in done else self.x)

    def outgoing(self, p, k, own=None):
        route = self.parts[p][2]
        region = self.held(p, route[:k], self.c)
        source = region if own is None else own
        if route[k] == "z":
            devices = [self.device(z=(self.z + j) % 4) for j in (1, 2, 3)]
        else:
            devices = [self.device(y=1 - self.y) if route[k] == "y" else self.device(x=1 - self.x)]
        return [self.remote(source, region, p, k, device) for device in devices]

    def arriving(self, p, k, c):
        route = self.parts[p][2]
        done = route[:k]
        z = ALL if "z" in done else self.z
        y = ALL if "y" in done else self.y
        x = None if "x" in done else self.x
        if route[k] == "z":
            return [self.region(p, (self.z + j) % 4, y, c, x) for j in (1, 2, 3)]
        if route[k] == "y":
            return [self.region(p, z, 1 - self.y, c, x)]
        return [self.region(p, z, y, c, 1 - self.x)]

    def amount(self, p, k):
        route = self.parts[p][2]
        if route[k] != "z":
            return self.held(p, route[:k], self.c)
        y = ALL if "y" in route[:k] else self.y
        return self.region(p, pl.ds(0, 3), y, self.c, None if "x" in route[:k] else self.x)

    def sibling(self, p, k, c):
        regions = [self.held(p, self.parts[p][2][:1], c)] if k == 0 else self.arriving(p, k, c)
        device = self.device(c=1 - self.c)
        return [self.remote(ref, ref, p, 3 + k, device) for ref in regions]

    def sibling_amount(self, p, k):
        ref = self.held(p, self.parts[p][2][:1], self.c) if k == 0 else self.amount(p, k)
        return self.remote(ref, ref, p, 3 + k, self.device(c=1 - self.c))

    def start(self, copies):
        for copy in copies:
            copy.start()

    def begin(self, p):
        self.place_own(p).start()
        self.start(self.outgoing(p, 0, self.shard(p)))

    def event(self, p, k):
        self.stage_amount(p, k).wait_recv()
        if k == 0:
            self.place_own(p).wait()
        if k < 2:
            self.start(self.outgoing(p, k + 1))
        self.start(self.sibling(p, k, self.c))

    def stage_amount(self, p, k):
        ref = self.amount(p, k)
        return self.remote(ref, ref, p, k, self.device(c=1 - self.c))

    def ready(self, p):
        for k in range(3):
            self.sibling_amount(p, k).wait_recv()

    def drain(self):
        for p in range(len(self.parts)):
            for k in range(3):
                self.stage_amount(p, k).wait_send()
                self.sibling_amount(p, k).wait_send()


class Exchange:
    def __init__(self, r, comm, name, index):
        self.comm, self.index = comm, index
        self.pack = getattr(r, "pack_" + name)
        self.swap = getattr(r, "swap_" + name)
        self.mine = getattr(r, "mine_" + name)
        self.terms = getattr(r, "terms_" + name)
        self.sums = getattr(r, "sums_" + name)
        self.send_sem, self.recv_sem = r.sum_send, r.sum_recv
        self.chip = comm.z * 2 + comm.y

    def remote(self, source, target, stage, device):
        return pltpu.make_async_remote_copy(
            source,
            target,
            self.send_sem.at[self.index, stage],
            self.recv_sem.at[self.index, stage],
            device_id=device,
            device_id_type=MESH,
        )

    def fill(self, sources):
        count = self.pack.shape[3]
        tile = 0
        for ref, width in sources:
            for row in range(ref.shape[0] // 8):
                for col in range(width // 128):
                    core, chip, slot = tile // (8 * count), tile // count % 8, tile % count
                    for x in range(2):
                        start = (x * width if ref.shape[1] > width else 0) + 128 * col
                        self.pack[x, core, chip, slot] = ref[8 * row : 8 * row + 8, start : start + 128]
                    tile += 1
        while tile < 16 * count:
            core, chip, slot = tile // (8 * count), tile // count % 8, tile % count
            for x in range(2):
                self.pack[x, core, chip, slot] = jnp.zeros((8, 128), f32)
            tile += 1

    def swap_copy(self):
        c = self.comm.c
        return self.remote(self.pack.at[:, 1 - c], self.swap, 0, self.comm.device(c=1 - c))

    def chip_copies(self):
        own = self.comm.x * 8 + self.chip
        for j in range(1, 16):
            index = (own + j) % 16
            x, chip = index // 8, index % 8
            yield self.remote(self.mine.at[x, chip], self.terms.at[own], 1, (chip * 2 + self.comm.c, x))

    def sum_copies(self):
        own = self.chip * 2 + self.comm.c
        slot = self.sums.at[own]
        for j in range(1, 16):
            yield self.remote(slot, slot, 2, ((own + j) % 16, self.comm.x))

    def all_copies(self, stage):
        ref = (self.terms if stage == 1 else self.sums).at[pl.ds(0, 15)]
        return self.remote(ref, ref, stage, self.comm.device(c=1 - self.comm.c))

    def start(self, sources):
        self.fill(sources)
        self.swap_copy().start()

    def spread(self):
        self.swap_copy().wait_recv()
        comm = self.comm
        for x in range(2):
            for chip in range(8):
                total = self.pack[x, comm.c, chip] + self.swap[x, chip]
                self.mine[x, chip] = total.reshape(self.mine.shape[2:]).astype(bf16)
        for copy in self.chip_copies():
            copy.start()
        self.terms[comm.x * 8 + self.chip] = self.mine[comm.x, self.chip]

    def add(self):
        self.all_copies(1).wait_recv()
        total = self.terms[0].astype(f32)
        for index in range(1, 16):
            total = total + self.terms[index].astype(f32)
        self.sums[self.chip * 2 + self.comm.c] = total.astype(bf16)
        for copy in self.sum_copies():
            copy.start()

    def collect(self):
        self.all_copies(2).wait_recv()

    def drain(self):
        self.swap_copy().wait_send()
        self.all_copies(1).wait_send()
        self.all_copies(2).wait_send()


def exchange_scratch(name, count):
    tiles = (count, 8, 128)
    return {
        "pack_" + name: ((2, 2, 8) + tiles, f32),
        "swap_" + name: ((2, 8) + tiles, f32),
        "mine_" + name: ((2, 8, count // 2, 16, 128), bf16),
        "terms_" + name: ((16, count // 2, 16, 128), bf16),
    }


PARTS = (
    ("embed", None, "zxy"),
    ("wqkv", 0, "zyx"),
    ("wqkv", 1, "zxy"),
    ("wqkv", 2, "zyx"),
    ("wout", None, "zyx"),
    ("wup", 0, "zxy"),
    ("wup", 1, "xzy"),
    ("wup", 2, "zyx"),
    ("wdown", 0, "zyx"),
    ("wdown", 1, "xyz"),
    ("wdown", 2, "zxy"),
)
PLAN = (
    ("b", 0),
    ("b", 1),
    ("b", 2),
    ("b", 3),
    ("b", 4),
    ("b", 5),
    ("b", 6),
    ("b", 7),
    ("b", 8),
    ("b", 9),
    ("b", 10),
    ("s", "prep0"),
    ("s", "prep1"),
    (0, 6),
    (0, 9),
    (0, 0),
    (0, 1),
    (1, 9),
    (1, 0),
    (0, 2),
    (1, 1),
    (0, 3),
    (1, 2),
    (0, 4),
    (2, 0),
    ("s", "pos0"),
    (1, 3),
    (0, 5),
    (2, 1),
    ("s", "pos1"),
    (0, 7),
    (2, 2),
    ("s", "pos2"),
    (2, 3),
    (0, 8),
    ("s", "pos3"),
    (1, 4),
    ("s", "qkv0"),
    ("s", "qkv1"),
    ("s", "qkv2"),
    ("s", "qkv3"),
    (1, 5),
    (0, 10),
    ("s", "qkv4"),
    (1, 7),
    ("s", "attend0.0"),
    ("s", "attend0.1"),
    ("s", "attend1.0"),
    (1, 8),
    ("s", "attend1.1"),
    (2, 4),
    ("s", "attend2.0"),
    ("s", "attend2.1"),
    (1, 6),
    ("s", "attend3.0"),
    (1, 10),
    ("s", "attend3.1"),
    ("s", "attend4.0"),
    (2, 5),
    ("s", "attend4.1"),
    ("s", "attend5.0"),
    ("s", "attend5.1"),
    ("s", "out"),
    (2, 7),
    ("s", "up0"),
    (2, 6),
    ("s", "up1"),
    ("s", "up2"),
    ("s", "up3"),
    (2, 9),
    ("s", "up4"),
    ("s", "up5"),
    (2, 8),
    ("s", "down"),
    ("s", "down0"),
    (2, 10),
    ("s", "down1"),
    ("s", "down2"),
)


STEPS = dict(
    prep0=(prepare_masks, ()),
    prep1=(prepare_factors, ()),
    pos0=(embed_positions, ("embed",)),
    pos1=(functools.partial(project_position, 0, False, "pq_far_t"), (("wqkv", 0),)),
    pos2=(functools.partial(project_position, 1, True, "pk_near_t"), (("wqkv", 1),)),
    pos3=(functools.partial(project_position, 1, False, "pk_far_t"), ()),
    qkv0=(reduce_tokens, ()),
    qkv1=(functools.partial(project_token, 0, "q"), ()),
    qkv2=(functools.partial(project_token, 1, "k"), ()),
    qkv3=(functools.partial(project_token, 2, "v"), (("wqkv", 2),)),
    qkv4=(arrange_heads, ()),
    attend=(attend, ()),
    out=(out_project, ("wout",)),
    up=(up_project, ()),
    down=(down_reduce, ()),
    down0=(functools.partial(down_third, 0), (("wdown", 0),)),
    down1=(functools.partial(down_third, 1), (("wdown", 1),)),
    down2=(functools.partial(down_third, 2), (("wdown", 2),)),
)
BACKWARD = (
    norm_two,
    down_back,
    up_back,
    out_back,
)


def run_plan(r, comm, plan):
    ready = set()
    waiting = []
    turns = {}
    counts = dict(attend=H, up=6)

    def act(items):
        for kind, arg in items:
            if kind == "r":
                comm.ready(arg)
            else:
                comm.event(arg, kind)

    def before(*turn):
        for place, items in turns.items():
            if items and place[1:] == turn[1:]:
                pl.when(turn[0] == place[0])(functools.partial(act, items))

    def need(parts):
        for p, part in enumerate(comm.parts):
            if p not in ready and (part[0] in parts or part[:2] in parts):
                ready.add(p)
                waiting.append(("r", p))

    for kind, arg in plan:
        if kind == "b":
            comm.begin(arg)
            continue
        if kind != "s":
            waiting.append((kind, arg))
            continue
        name = arg.rstrip("0123456789.")
        if name not in counts:
            step, needs = STEPS[arg]
            need(needs)
            act(waiting)
            waiting.clear()
            step(r)
            continue
        turn = tuple(int(c) for c in arg[len(name) :].split("."))
        if name == "up":
            need((("wup", turn[0] // 2),))
        turns[turn] = list(waiting)
        waiting.clear()
        if len(turns) == counts[name]:
            STEPS[name][0](r, before)
            turns = {}
    act(waiting)


EARLY, LATE = 4, 2
SUMS = dict(
    sums_early=((16, EARLY // 2, 16, 128), bf16), sums_late=((16, LATE // 2, 16, 128), bf16)
)
FUSED_SCRATCH = {
    **SCRATCH,
    **GATHERED,
    **GRADS,
    **exchange_scratch("early", EARLY),
    **exchange_scratch("late", LATE),
}


def layer_kernel(fused, *refs):
    r = Refs()
    if fused:
        names = INPUTS + SHARDS + OUTPUTS + list(SUMS) + list(FUSED_SCRATCH)
        names += ["load_sem", "send_sem", "recv_sem", "local_sem", "sum_send", "sum_recv"]
    else:
        names = INPUTS + list(GATHERED) + OUTPUTS + list(GRADS) + list(SCRATCH) + ["load_sem"]
    for name, ref in zip(names, refs, strict=True):
        setattr(r, name, ref)
    for name, target in ALIASES.items():
        setattr(r, name, getattr(r, target))
    if not fused:
        r.grad_lam[...] = jnp.zeros_like(r.grad_lam)
        for step, _ in STEPS.values():
            step(r)
        for step in BACKWARD + (attend_back, qkv_factors, qkv_input, finish_layer, finish_grad):
            step(r)
        return

    comm = Gather(r)
    comm.greet()
    r.grad_lam[...] = jnp.zeros_like(r.grad_lam)
    run_plan(r, comm, PLAN)
    for step in BACKWARD:
        step(r)
    early = Exchange(r, comm, "early", 0)
    late = Exchange(r, comm, "late", 1)
    early.start(((r.grad_wide, FF // 2), (r.grad_narrow, D // 2), (r.grad_fourth, D // 2)))

    def before(p):
        pl.when(p == 1)(early.spread)
        pl.when(p == 4)(early.add)

    attend_back(r, before)
    qkv_factors(r)
    late.start(((r.grad_attn, D // 2), (r.grad_lam, 128)))
    finish_layer(r)
    late.spread()
    qkv_input(r)
    finish_grad(r)
    comm.drain()
    early.collect()
    early.drain()
    late.add()
    late.collect()
    late.drain()


OUT_SHAPES = dict(layer_out=((L, D), bf16), grad_tokens=((L, D), bf16), **SUMS, **GRADS)


def unpack_kernel(layer_in, grad_in, early, late, layer_out, grad_out, ap, aq, upp, upq, dnp, dnq, glam, *parts):
    layer_out[...] = layer_in[...]
    grad_out[...] = grad_in[...]
    wide, narrow, fourth, attn = parts
    for sums, refs in ((early, (wide, narrow, fourth)), (late, (attn,))):
        count = 2 * sums.shape[1]
        tile = 0
        for ref in refs:
            for row in range(ref.shape[0] // 8):
                for col in range(ref.shape[1] // 128):
                    core, chip, slot = tile // (8 * count), tile // count % 8, tile % count
                    pair = sums[chip * 2 + core, slot // 2].astype(f32)
                    half = slice(8 * (slot % 2), 8 * (slot % 2) + 8)
                    ref[8 * row : 8 * row + 8, 128 * col : 128 * col + 128] = pair[half, :]
                    tile += 1
    core, chip, slot = tile // (8 * count), tile // count % 8, tile % count
    lam = sums[chip * 2 + core, slot // 2].astype(f32)[8 * (slot % 2) : 8 * (slot % 2) + 8, :]
    for n in range(4):
        glam[n : n + 1, :] = lam[0:1, R * n : R * (n + 1)]
    glam[4:6, :] = lam[4:6, 0:R]
    upp[...] = wide[:R, :]
    dnq[...] = wide[R:, :]
    upq[...] = narrow[:R, :]
    dnp[...] = narrow[R:, :]
    for n in range(3):
        ap[:, n, :] = attn[R * n : R * (n + 1), :]
        aq[:, n, :] = attn[3 * R + R * n : 3 * R + R * (n + 1), :]
    ap[:, 3, :] = fourth[:R, :]
    aq[:, 3, :] = fourth[R:, :]


def unpack_call(layer_out, grad_tokens, early, late):
    half = D // 2
    vmem = pl.BlockSpec(memory_space=pltpu.VMEM)
    shapes = [
        ((L, D), bf16),
        ((L, D), bf16),
        ((R, 4, half), f32),
        ((R, 4, half), f32),
        ((R, FF // 2), f32),
        ((R, half), f32),
        ((R, half), f32),
        ((R, FF // 2), f32),
        ((6, R), f32),
    ]
    return pl.pallas_call(
        unpack_kernel,
        out_shape=[jax.ShapeDtypeStruct(*shape) for shape in shapes],
        in_specs=[vmem] * 4,
        out_specs=[vmem] * len(shapes),
        scratch_shapes=[
            pltpu.VMEM((2 * R, FF // 2), f32),
            pltpu.VMEM((2 * R, half), f32),
            pltpu.VMEM((2 * R, half), f32),
            pltpu.VMEM((6 * R, half), f32),
        ],
    )(layer_out, grad_tokens, early, late)


def arrange_weight(weight, shape):
    *lead, rows, cols = weight.shape
    if shape[-1] == THIRD:
        split = weight.reshape(rows, 2, 3, THIRD)
        return jnp.transpose(split, (2, 1, 0, 3)).reshape(shape)
    split = weight.reshape(*lead, rows, 2, cols // 2)
    return jnp.moveaxis(split, -2, len(lead)).reshape(shape)


def layer_call(args, weights, fused):
    vmem = pl.BlockSpec(memory_space=pltpu.VMEM)
    hbm = pl.BlockSpec(memory_space=pl.ANY)
    load_sem = pltpu.SemaphoreType.DMA((2,))
    if fused:
        outputs = OUTPUTS + list(SUMS)
        scratch = [pltpu.VMEM(*spec) for spec in FUSED_SCRATCH.values()] + [
            load_sem,
            pltpu.SemaphoreType.DMA((len(PARTS), SLOTS)),
            pltpu.SemaphoreType.DMA((len(PARTS), SLOTS)),
            pltpu.SemaphoreType.DMA((len(PARTS),)),
            pltpu.SemaphoreType.DMA((2, 3)),
            pltpu.SemaphoreType.DMA((2, 3)),
        ]
        extra = dict(collective_id=0, has_side_effects=True)
    else:
        outputs = OUTPUTS + list(GRADS)
        scratch = [pltpu.VMEM(*spec) for spec in SCRATCH.values()] + [load_sem]
        weights = [arrange_weight(w, GATHERED[name][0]) for name, w in zip(GATHERED, weights)]
        extra = {}
    return pl.pallas_call(
        functools.partial(layer_kernel, fused),
        out_shape=[jax.ShapeDtypeStruct(*OUT_SHAPES[name]) for name in outputs],
        in_specs=[hbm if name in IN_HBM else vmem for name in INPUTS]
        + [hbm if fused else vmem] * len(weights),
        out_specs=[vmem] * len(outputs),
        scratch_shapes=scratch,
        compiler_params=pltpu.CompilerParams(vmem_limit_bytes=63 * 2**20, **extra),
    )(*args, *weights)


def gather_plain(w_qkv, w_out, w_up, down_t, rel_embed):
    parts = []
    for shard, rows, cols in (
        (w_qkv, 1, 2),
        (w_out, 0, 1),
        (w_up, 0, 1),
        (down_t, 0, 1),
        (rel_embed, 0, 1),
    ):
        part = lax.all_gather(shard, "inner", axis=cols, tiled=True)
        parts.append(lax.all_gather(part, "group", axis=rows, tiled=True))
    return parts


def reduce_plain(grads):
    shared = [
        lax.psum(lax.psum_scatter(g, "inner", scatter_dimension=1, tiled=True), "group")
        for g in grads[:-1]
    ]
    return shared, lax.psum(grads[-1], ("group", "inner"))


def on_device(
    tokens,
    cotangent,
    segments,
    w_qkv,
    w_out,
    w_up,
    w_down,
    rel_embed,
    attn_bias,
    up_bias,
    down_bias,
    norm_gain,
    norm_bias,
    attn_p,
    attn_q,
    up_p,
    up_q,
    down_p,
    down_q,
    lam,
):
    fused = (lax.axis_size("group"), lax.axis_size("inner")) == (16, 2)
    down_t = jnp.transpose(w_down)
    weights = (w_qkv, w_out, w_up, down_t, rel_embed)
    if not fused:
        weights = gather_plain(*weights)
    args = (
        tokens,
        cotangent,
        segments,
        jnp.asarray(bucket_rows()),
        attn_bias,
        up_bias,
        down_bias,
        norm_gain,
        norm_bias,
        jnp.transpose(attn_p, (2, 1, 0)),
        jnp.transpose(attn_q, (2, 1, 0)),
        up_p.T,
        up_q.T,
        down_p.T,
        down_q.T,
        lam,
    )
    layer_out, grad_tokens, *sums = layer_call(args, weights, fused)
    if fused:
        layer_out, grad_tokens, ap, aq, upp, upq, dnp, dnq, grad_lam = unpack_call(
            layer_out, grad_tokens, *sums
        )
    else:
        (wide, narrow, fourth, attn), lam_sums = reduce_plain(sums)
        by_rank = [attn[R * n : R * (n + 1)] for n in range(6)]
        ap = jnp.stack(by_rank[:3] + [fourth[:R]], axis=1)
        aq = jnp.stack(by_rank[3:] + [fourth[R:]], axis=1)
        upp, dnq, upq, dnp = wide[:R], wide[R:], narrow[:R], narrow[R:]
        grad_lam = jnp.concatenate([lam_sums[0, : 4 * R].reshape(4, R), lam_sums[4:6, :R]], axis=0)
    return (
        layer_out,
        grad_tokens,
        jnp.transpose(ap, (2, 1, 0)),
        jnp.transpose(aq, (2, 1, 0)),
        upp.T,
        upq.T,
        dnp.T,
        dnq.T,
        grad_lam,
    )


def solution(mesh):
    rows = P(("group", "inner"), None)
    return jax.shard_map(
        on_device,
        mesh=mesh,
        in_specs=(
            rows,
            rows,
            rows,
            P(None, "group", "inner"),
            P("group", "inner"),
            P("group", "inner"),
            P("inner", "group"),
            P("group", "inner"),
        )
        + (P(),) * 12,
        out_specs=(
            rows,
            rows,
            P("inner", None, None),
            P("inner", None, None),
            P("inner", None),
            P("inner", None),
            P("inner", None),
            P("inner", None),
            P(),
        ),
        check_vma=False,
    )
```

```python
import functools

import jax
import jax.numpy as jnp
import numpy as np
from jax import lax
from jax.experimental import pallas as pl
from jax.experimental.pallas import tpu as pltpu
from jax.sharding import PartitionSpec as P

D = 768
H = 12
DH = 64
FF = 3072
SPAN = 256
L = 512
R = 12
HALF = L // 2
SCALE = (3.0 * DH) ** (-0.5)
EPS = 1e-07

bf16 = jnp.bfloat16
f32 = jnp.float32


def bucket_values(offsets, span_size):
    middle = span_size // 2
    magnitude = np.abs(offsets)
    inside = magnitude <= middle
    clipped = np.maximum(magnitude, middle) * 1.0
    logged = (
        np.ceil(np.log(clipped / middle) / np.log((2 * span_size - 1) / middle) * (middle - 1))
        + middle
    )
    bucket = np.where(inside, offsets, np.sign(offsets) * logged.astype(np.int32))
    return np.clip(bucket + span_size, 0, 2 * span_size - 1).astype(np.int32)


def bucket_rows():
    offsets = np.minimum(np.arange(2 * HALF) - (HALF - 1), HALF - 1)
    far = bucket_values(offsets, SPAN)
    near = bucket_values(-offsets, SPAN)
    return np.stack([near, far]).astype(np.int32)


def mm(a, b):
    return lax.dot_general(a, b, (((1,), (0,)), ((), ())), preferred_element_type=f32)


def mm_t(a, b):
    return lax.dot_general(a, b, (((1,), (1,)), ((), ())), preferred_element_type=f32)


def tmm(a, b):
    return lax.dot_general(a, b, (((0,), (0,)), ((), ())), preferred_element_type=f32)


def iota(shape, dim):
    return lax.broadcasted_iota(jnp.int32, shape, dim)


def loop(count, body):
    def step(index, carry):
        body(index)
        return carry

    lax.fori_loop(0, count, step, 0)


def block(index, size):
    return pl.ds(pl.multiple_of(index * size, size), size)


def mean_row(values):
    return jnp.sum(values, axis=1, keepdims=True) * (1.0 / D)


def flat(block):
    return block.reshape(-1, block.shape[-1])


def whole(ref):
    return jnp.concatenate([flat(ref[x]) for x in range(2)], axis=1)


THIRD = FF // 6


def whole_wide(ref):
    return jnp.concatenate([flat(ref[t, x]) for x in range(2) for t in range(3)], axis=1)


def third(t, x):
    return pl.ds(pl.multiple_of((3 * x + t) * THIRD, THIRD), THIRD)


SCRATCH = dict(
    shift=((L, L), bf16),
    unshift=((L, L), bf16),
    flip=((HALF, HALF), bf16),
    mask=((2, HALF, HALF), f32),
    tok=((L, D), bf16),
    cot=((L, D), bf16),
    pk_near_t=((D, L), bf16),
    pk_far_t=((D, L), bf16),
    pq_far_t=((D, L), bf16),
    emb_near=((L, D), bf16),
    emb_far=((L, D), bf16),
    q=((L, D), bf16),
    k=((L, D), bf16),
    v=((L, D), bf16),
    qt=((D, L), bf16),
    kt=((D, L), bf16),
    k_rev_t=((D, L), bf16),
    g_t=((D, L), bf16),
    v_rev=((L, D), bf16),
    v_rev_t=((D, L), bf16),
    probs=((H, L, HALF), bf16),
    probs_t=((H, L, HALF), bf16),
    ctx=((L, D), bf16),
    attn_pt=((4 * R, D), bf16),
    attn_qt=((4 * R, D), bf16),
    up_pt=((R, FF), bf16),
    up_qt=((R, D), bf16),
    down_pt=((R, D), bf16),
    down_qt=((R, FF), bf16),
    lam_row=((8, 4 * R), f32),
    lam_col=((4 * R, 1), f32),
    up_row=((1, FF), f32),
    down_row=((1, D), f32),
    u_t=((4 * R, L), f32),
    du_t=((4 * R, L), bf16),
    u_pos_t=((4 * R, L), f32),
    u_up_t=((R, L), f32),
    u_down_t=((R, L), f32),
    xhat1=((L, D), f32),
    rs1=((L, 1), f32),
    hidden=((L, D), f32),
    hid=((L, D), bf16),
    act=((L, FF), bf16),
    slope=((L, FF), bf16),
    branch=((L, D), f32),
    gsum2=((L, D), f32),
    gb5=((L, D), bf16),
    gpk_t=((D, L), bf16),
    gpq_t=((D, L), bf16),
)

GATHERED = dict(
    wqkv=((3, 2, 4, 2, 2, 48, D // 2), bf16),
    wout=((2, 4, 2, 2, 48, D // 2), bf16),
    wup=((3, 2, 4, 2, 2, 48, THIRD), bf16),
    wdown=((3, 2, 4, 2, 2, 48, THIRD), bf16),
    embed=((2, 4, 2, 2, 32, D // 2), bf16),
)

ALIASES = dict(
    gpre="slope",
    gsum1="gsum2",
    gb3="gb5",
    gctx="q",
    gq_t="kt",
    gk_t="pk_near_t",
    gv_t="v_rev_t",
    low_out="layer_out",
)

INPUTS = [
    "tokens",
    "cotangent",
    "segments",
    "buckets",
    "attn_bias",
    "up_bias",
    "down_bias",
    "norm_gain",
    "norm_bias",
    "attn_p",
    "attn_q",
    "up_p",
    "up_q",
    "down_p",
    "down_q",
    "lam",
]
SHARDS = [name + "_shard" for name in GATHERED]
IN_HBM = ["tokens", "cotangent"]
OUTPUTS = ["layer_out", "grad_tokens"]
GRADS = dict(
    grad_wide=((2 * R, FF), f32),
    grad_narrow=((2 * R, D), f32),
    grad_fourth=((2 * R, D), f32),
    grad_attn=((6 * R, D), f32),
    grad_lam=((8, 128), f32),
)


class Refs:
    pass


def as_column(row):
    return jnp.transpose(jnp.broadcast_to(row, (128, row.shape[1])))[:, 0:1]


def rank_group(n):
    rank = iota((4 * R, 1), 0)
    return ((rank >= R * n) & (rank < R * (n + 1))).astype(f32)


def prepare_masks(r):
    seg_row = r.segments[...]
    seg_col = as_column(seg_row)
    same = (seg_col == seg_row).astype(f32)
    width = jnp.sum(same, axis=0, keepdims=True)
    place = iota((1, L), 1).astype(f32)
    start = jnp.min(jnp.where(width == float(HALF), place, float(L)), axis=1, keepdims=True)
    row, col = iota((L, L), 0).astype(f32), iota((L, L), 1).astype(f32)
    ahead = row + start
    ahead = jnp.where(ahead >= float(L), ahead - float(L), ahead)
    r.shift[...] = (col == ahead).astype(bf16)
    back = col + start
    back = jnp.where(back >= float(L), back - float(L), back)
    r.unshift[...] = (row == back).astype(bf16)
    r.flip[...] = (iota((HALF, HALF), 0) + iota((HALF, HALF), 1) == HALF - 1).astype(bf16)
    seg_low = jnp.broadcast_to(seg_row.astype(f32), (8, L)).astype(bf16)
    moved_row = mm_t(seg_low, r.shift[...])[0:1, :]
    moved_col = as_column(moved_row)
    for b in range(2):
        rows = slice(HALF * b, HALF * (b + 1))
        r.mask[b] = jnp.where(moved_col[rows, :] == moved_row[:, rows], 0.0, -1e30)


def prepare_factors(r):
    copies = [
        pltpu.make_async_copy(source, target, r.load_sem.at[i])
        for i, (source, target) in enumerate(((r.tokens, r.tok), (r.cotangent, r.cot)))
    ]
    for copy in copies:
        copy.start()
    r.attn_pt[...] = jnp.concatenate([r.attn_p[:, n, :] for n in range(4)], axis=0).astype(bf16)
    r.attn_qt[...] = jnp.concatenate([r.attn_q[:, n, :] for n in range(4)], axis=0).astype(bf16)
    r.up_pt[...] = r.up_p[...].astype(bf16)
    r.up_qt[...] = r.up_q[...].astype(bf16)
    r.down_pt[...] = r.down_p[...].astype(bf16)
    r.down_qt[...] = r.down_q[...].astype(bf16)
    for n in range(4):
        r.lam_row[0:1, R * n : R * (n + 1)] = r.lam[n : n + 1, :]
    r.lam_col[...] = as_column(r.lam_row[0:1, :])
    r.up_row[...] = r.up_bias[...].astype(f32).reshape(1, FF)
    r.down_row[...] = r.down_bias[...].astype(f32).reshape(1, D)
    copies[0].wait()
    r.tok[...] = mm(r.shift[...], r.tok[...]).astype(bf16)
    copies[1].wait()
    r.cot[...] = mm(r.shift[...], r.cot[...]).astype(bf16)


def embed_positions(r):
    column = iota((L, L), 1)
    near_table, far_table = ((as_column(r.buckets[i : i + 1, :]) == column).astype(bf16) for i in range(2))
    r.emb_near[...] = mm(near_table, whole(r.embed)).astype(bf16)
    r.emb_far[...] = mm(far_table, whole(r.embed)).astype(bf16)
    r.u_pos_t[...] = mm_t(r.attn_qt[...], r.emb_far[...])


def project_position(n, near, out, r):
    emb = r.emb_near if near else r.emb_far
    u = mm_t(r.attn_qt[...], emb[...]) if near else r.u_pos_t[...]
    mixed_t = (u * r.lam_col[...] * rank_group(n)).astype(bf16)
    result = (
        mm(emb[...], whole(r.wqkv.at[n]))
        + r.attn_bias[n : n + 1, :].astype(f32)
        + tmm(mixed_t, r.attn_pt[...])
    ).astype(bf16)
    getattr(r, out)[...] = jnp.transpose(result)


def reduce_tokens(r):
    r.u_t[...] = mm_t(r.attn_qt[...], r.tok[...])


def project_token(n, out, r):
    mixed_t = (r.u_t[...] * r.lam_col[...] * rank_group(n)).astype(bf16)
    getattr(r, out)[...] = (
        mm(r.tok[...], whole(r.wqkv.at[n]))
        + r.attn_bias[n : n + 1, :].astype(f32)
        + tmm(mixed_t, r.attn_pt[...])
    ).astype(bf16)


def flip_columns(r, source, target):
    for b in range(2):
        cols = slice(HALF * b, HALF * (b + 1))
        target[:, cols] = mm(source[:, cols], r.flip[...]).astype(bf16)


def arrange_heads(r):
    for b in range(2):
        rows = slice(HALF * b, HALF * (b + 1))
        r.v_rev[rows, :] = mm(r.flip[...], r.v[rows, :]).astype(bf16)
    r.v_rev_t[...] = jnp.transpose(r.v_rev[...])
    r.qt[...] = jnp.transpose(r.q[...])
    r.kt[...] = jnp.transpose(r.k[...])
    flip_columns(r, r.kt, r.k_rev_t)


def head_lanes(a):
    lane = iota((1, 2 * DH), 1)
    return ((lane >= DH) if a else (lane < DH)).astype(bf16)


def attend(r, before=None):
    def pair(p):
        cols = block(p, 2 * DH)
        high = iota((HALF, HALF), 1) + iota((HALF, HALF), 0) >= HALF - 1
        for b in range(2):
            if before is not None:
                before(p, b)
            rows = slice(HALF * b, HALF * (b + 1))
            q, k, v = r.q[rows, cols], r.k[rows, cols], r.v[rows, cols]
            keys = r.kt[cols, rows]
            near_keys, far_queries = r.pk_near_t[cols, :], r.pq_far_t[cols, :]
            probs = []
            for a in range(2):
                lanes = head_lanes(a)
                qa, ka = q * lanes, k * lanes
                content, to, fro = mm(qa, keys), mm(qa, near_keys), mm(ka, far_queries)
                near = jnp.where(high, to[:, :HALF], to[:, HALF:])
                near = pltpu.roll(near, 1, 1, stride=1, stride_axis=0)
                far = jnp.where(high, fro[:, :HALF], fro[:, HALF:])
                far = pltpu.roll(far, 1, 1, stride=1, stride_axis=0)
                scores = (content + near + jnp.transpose(far)) * SCALE + r.mask[b]
                peak = jnp.max(scores, axis=1, keepdims=True)
                terms = jnp.exp(scores - peak)
                total = jnp.sum(terms, axis=1, keepdims=True)
                probs.append((terms * (1.0 / total)).astype(bf16))
            context = mm(probs[0], v * head_lanes(0)) + mm(probs[1], v * head_lanes(1))
            turned = [mm(probs[a], r.flip[...]).astype(bf16) for a in range(2)]
            turned_t = [jnp.transpose(turned[a]) for a in range(2)]
            for a in range(2):
                r.probs[2 * p + a, rows, :] = turned[a]
                r.probs_t[2 * p + a, rows, :] = turned_t[a]
            r.ctx[rows, cols] = context.astype(bf16)

    loop(H // 2, pair)


def out_project(r):
    ctx = r.ctx[...]
    u = mm_t(r.attn_qt[...], ctx)
    r.u_t[3 * R :, :] = u[3 * R :, :]
    mixed_t = (u * r.lam_col[...] * rank_group(3)).astype(bf16)
    r.hidden[...] = (
        mm(ctx, whole(r.wout))
        + r.attn_bias[3:4, :].astype(f32)
        + tmm(mixed_t, r.attn_pt[...])
    )
    gain, bias = r.norm_gain[0:1, :].astype(f32), r.norm_bias[0:1, :].astype(f32)

    def part(i):
        rows = block(i, 128)
        total = r.tok[rows, :].astype(f32) + r.hidden[rows, :]
        centre = total - mean_row(total)
        rs = lax.rsqrt(mean_row(centre * centre) + EPS)
        xhat = centre * rs
        hidden = xhat * gain + bias
        r.xhat1[rows, :] = xhat
        r.rs1[rows, :] = rs
        r.hidden[rows, :] = hidden
        r.hid[rows, :] = hidden.astype(bf16)

    loop(L // 128, part)
    r.u_up_t[...] = mm_t(r.up_qt[...], r.hid[...])


def up_project(r, before=None):
    def part(i):
        if before is not None:
            before(i)
        up_block(r, i // 2, i % 2)

    loop(6, part)


def up_block(r, t, x):
    cols = third(t, x)
    mixed_t = (r.u_up_t[...] * as_column(r.lam[4:5, :])).astype(bf16)
    pre = (
        mm(r.hid[...], flat(r.wup[t, x]))
        + r.up_row[:, cols]
        + tmm(mixed_t, r.up_pt[:, cols])
    )
    phi = 0.5 * (1.0 + lax.erf(pre * np.float32(np.sqrt(0.5))))
    r.act[:, cols] = (pre * phi).astype(bf16)
    bell = jnp.exp(-0.5 * pre * pre) * np.float32(1.0 / np.sqrt(2.0 * np.pi))
    r.slope[:, cols] = (phi + pre * bell).astype(bf16)


def down_reduce(r):
    r.u_down_t[...] = mm_t(r.down_qt[...], r.act[...])
    mixed_t = (r.u_down_t[...] * as_column(r.lam[5:6, :])).astype(bf16)
    r.branch[...] = r.down_row[...] + tmm(mixed_t, r.down_pt[...])


def down_third(t, r):
    act = jnp.concatenate([r.act[:, third(t, x)] for x in range(2)], axis=1)
    weight = jnp.concatenate([flat(r.wdown[t, x]) for x in range(2)], axis=1)
    r.branch[...] += mm_t(act, weight)


def norm_two(r):
    gain, bias = r.norm_gain[1:2, :].astype(f32), r.norm_bias[1:2, :].astype(f32)

    def part(i):
        rows = block(i, 128)
        total = r.hidden[rows, :] + r.branch[rows, :]
        centre = total - mean_row(total)
        rs = lax.rsqrt(mean_row(centre * centre) + EPS)
        xhat = centre * rs
        r.low_out[rows, :] = (xhat * gain + bias).astype(bf16)
        e = r.cot[rows, :].astype(f32) * gain
        grad = rs * (e - mean_row(e) - xhat * mean_row(e * xhat))
        r.gsum2[rows, :] = grad
        r.gb5[rows, :] = grad.astype(bf16)

    loop(L // 128, part)


def back_factors(gb, p_t, u_t, lam):
    dmixed = mm_t(p_t, gb)
    return mm((u_t * lam).astype(bf16), gb), (dmixed * lam).astype(bf16), dmixed * u_t


def as_row(column):
    return jnp.transpose(jnp.broadcast_to(column, (column.shape[0], 128)))[0:1, :]


def down_back(r):
    gb = r.gb5[...]
    dp, du, dlam = back_factors(gb, r.down_pt[...], r.u_down_t[...], as_column(r.lam[5:6, :]))
    r.grad_narrow[R:, :] = dp
    r.grad_lam[5:6, 0:R] = as_row(jnp.sum(dlam, axis=1, keepdims=True))[:, 0:R]

    def part(t):
        for x in range(2):
            cols = third(t, x)
            grad = mm(gb, flat(r.wdown[t, x])) + tmm(du, r.down_qt[:, cols])
            r.grad_wide[R:, cols] = mm(du, r.act[:, cols])
            r.gpre[:, cols] = (grad * r.slope[:, cols].astype(f32)).astype(bf16)

    loop(3, part)


def up_back(r):
    gb = r.gpre[...]
    dp, du, dlam = back_factors(gb, r.up_pt[...], r.u_up_t[...], as_column(r.lam[4:5, :]))
    r.grad_wide[:R, :] = dp
    r.grad_lam[4:5, 0:R] = as_row(jnp.sum(dlam, axis=1, keepdims=True))[:, 0:R]
    r.grad_narrow[:R, :] = mm(du, r.hid[...])
    r.branch[...] = mm_t(gb, whole_wide(r.wup)) + tmm(du, r.up_qt[...])
    gain = r.norm_gain[0:1, :].astype(f32)

    def part(i):
        rows = block(i, 128)
        e = (r.gsum2[rows, :] + r.branch[rows, :]) * gain
        xhat = r.xhat1[rows, :]
        grad = r.rs1[rows, :] * (e - mean_row(e) - xhat * mean_row(e * xhat))
        r.gsum1[rows, :] = grad
        r.gb3[rows, :] = grad.astype(bf16)

    loop(L // 128, part)


def out_back(r):
    gb = r.gb3[...]
    dp, du, dlam = back_factors(gb, r.attn_pt[...], r.u_t[...], r.lam_col[...] * rank_group(3))
    r.grad_fourth[:R, :] = dp[3 * R :, :]
    r.grad_fourth[R:, :] = mm(du, r.ctx[...])[3 * R :, :]
    r.grad_lam[0:1, 0 : 4 * R] = as_row(jnp.sum(dlam * rank_group(3), axis=1, keepdims=True))
    r.gctx[...] = (mm_t(gb, whole(r.wout)) + tmm(du, r.attn_qt[...])).astype(bf16)
    r.g_t[...] = jnp.transpose(r.gctx[...])


def attend_back(r, before=None):
    def pair(p):
        if before is not None:
            before(p)
        cols = block(p, 2 * DH)
        low = iota((HALF, HALF), 1) >= iota((HALF, HALF), 0)
        zero = jnp.zeros((HALF, HALF), bf16)
        units = [(a, b) for a in range(2) for b in range(2)]
        part = [slice(HALF * b, HALF * (b + 1)) for b in range(2)]
        feats = [block(2 * p + a, DH) for a in range(2)]
        ready, stores = {}, []
        for a, b in units:
            rows, head, lanes = part[b], 2 * p + a, head_lanes(a)
            gprobs = mm(r.gctx[rows, cols] * lanes, r.v_rev_t[cols, rows])
            gprobs_t = mm(r.v_rev[rows, cols] * lanes, r.g_t[cols, rows])
            probs = r.probs[head, rows, :].astype(f32)
            delta = jnp.sum(probs * gprobs, axis=1, keepdims=True)
            gs = (probs * (gprobs - delta)).astype(bf16)
            probs_t = r.probs_t[head, rows, :].astype(f32)
            delta_t = jnp.sum(probs_t * gprobs_t, axis=0, keepdims=True)
            gs_t = (probs_t * (gprobs_t - delta_t)).astype(bf16)
            ready[a, b] = gs, gs_t
        for a in range(2):
            gpk = gpq = None
            for b in range(2):
                rows = part[b]
                gs, gs_t = ready[a, b]
                turn = pltpu.roll(gs, 0, 1, stride=1, stride_axis=0)
                to = jnp.concatenate([jnp.where(low, turn, zero), jnp.where(low, zero, turn)], axis=1)
                turn_t = pltpu.roll(gs_t, 0, 1, stride=1, stride_axis=0)
                fro = jnp.concatenate([jnp.where(low, turn_t, zero), jnp.where(low, zero, turn_t)], axis=1)
                queries, keys = r.qt[feats[a], rows], r.k_rev_t[feats[a], rows]
                query_part = mm(queries, jnp.concatenate([gs, to], axis=1))
                key_part = mm(keys, jnp.concatenate([gs_t, fro], axis=1))
                gk = query_part[:, :HALF] + mm_t(r.pq_far_t[feats[a], :], fro)
                gv = mm(r.g_t[feats[a], rows], r.probs[2 * p + a, rows, :])
                gq = key_part[:, :HALF] + mm_t(r.pk_far_t[feats[a], :], to)
                gpk_b, gpq_b = query_part[:, HALF:], key_part[:, HALF:]
                gpk = gpk_b if gpk is None else gpk + gpk_b
                gpq = gpq_b if gpq is None else gpq + gpq_b
                stores.append((r.gq_t, feats[a], rows, gq * SCALE))
                stores.append((r.gk_t, feats[a], rows, gk * SCALE))
                stores.append((r.gv_t, feats[a], rows, gv))
            stores.append((r.gpk_t, feats[a], slice(None), gpk * SCALE))
            stores.append((r.gpq_t, feats[a], slice(None), gpq * SCALE))
        for ref, feat, rows, value in stores:
            ref[feat, rows] = value.astype(bf16)

    loop(H // 2, pair)


def qkv_factors(r):
    flip_columns(r, r.gk_t, r.gk_t)
    flip_columns(r, r.gv_t, r.gv_t)
    lam = r.lam_col[...]
    u = r.u_t[...]
    dmixed = jnp.zeros((4 * R, L), f32)
    ap = jnp.zeros((4 * R, D), f32)
    for n, g in ((0, r.gq_t), (1, r.gk_t), (2, r.gv_t)):
        gb = g[...]
        dmixed += mm(r.attn_pt[...], gb) * rank_group(n)
        ap += mm_t((u * lam * rank_group(n)).astype(bf16), gb)
    du = (dmixed * lam).astype(bf16)
    r.du_t[...] = du
    aq = mm(du, r.tok[...])
    lam_grad = dmixed * u
    u = r.u_pos_t[...]
    for n, grads in ((0, r.gpq_t), (1, r.gpk_t)):
        gb = grads[...]
        dmixed = mm(r.attn_pt[...], gb) * rank_group(n)
        ap += mm_t((u * lam * rank_group(n)).astype(bf16), gb)
        aq += mm((dmixed * lam).astype(bf16), r.emb_far[...])
        lam_grad += dmixed * u
    r.grad_attn[: 3 * R, :] = ap[: 3 * R, :]
    r.grad_attn[3 * R :, :] = aq[: 3 * R, :]
    r.grad_lam[0:1, 0 : 4 * R] += as_row(jnp.sum(lam_grad, axis=1, keepdims=True))


def qkv_input(r):
    grad_t = tmm(r.attn_qt[...], r.du_t[...])
    for n, g in ((0, r.gq_t), (1, r.gk_t), (2, r.gv_t)):
        grad_t += mm(whole(r.wqkv.at[n]), g[...])
    r.gsum1[...] += jnp.transpose(grad_t)


def finish_layer(r):
    r.layer_out[...] = mm(r.unshift[...], r.low_out[...]).astype(bf16)


def finish_grad(r):
    r.grad_tokens[...] = mm(r.unshift[...], r.gsum1[...].astype(bf16)).astype(bf16)


MESH = pl.DeviceIdType.MESH
SLOTS = 6
ALL = slice(None)


class Gather:
    def __init__(self, r):
        self.r, self.parts = r, PARTS
        group = lax.axis_index("group")
        self.x = lax.axis_index("inner")
        self.z, self.y, self.c = group // 4, (group // 2) % 2, group % 2

    def device(self, x=None, y=None, z=None, c=None):
        x = self.x if x is None else x
        y = self.y if y is None else y
        z = self.z if z is None else z
        c = self.c if c is None else c
        return ((z * 2 + y) * 2 + c, x)

    def greet(self):
        barrier = pltpu.get_barrier_semaphore()
        partners = [self.device(x=1 - self.x), self.device(y=1 - self.y), self.device(c=1 - self.c)]
        partners += [self.device(z=(self.z + j) % 4) for j in (1, 2, 3)]
        for partner in partners:
            pl.semaphore_signal(barrier, inc=1, device_id=partner, device_id_type=MESH)
        pl.semaphore_wait(barrier, len(partners))

    def region(self, p, z, y, c, x):
        name, lead, _ = self.parts[p]
        ref = getattr(self.r, name)
        ref = ref if lead is None else ref.at[lead]
        return ref.at[ALL if x is None else x, z, y, c]

    def shard(self, p):
        name, lead, _ = self.parts[p]
        ref = getattr(self.r, name + "_shard")
        if lead is None:
            return ref
        return ref.at[lead] if name == "wqkv" else ref.at[:, pl.ds(lead * THIRD, THIRD)]

    def remote(self, source, target, p, slot, device):
        return pltpu.make_async_remote_copy(
            source,
            target,
            self.r.send_sem.at[p, slot],
            self.r.recv_sem.at[p, slot],
            device_id=device,
            device_id_type=MESH,
        )

    def place_own(self, p):
        target = self.region(p, self.z, self.y, self.c, self.x)
        return pltpu.make_async_copy(self.shard(p), target, self.r.local_sem.at[p])

    def held(self, p, done, c):
        z = ALL if "z" in done else self.z
        y = ALL if "y" in done else self.y
        return self.region(p, z, y, c, None if "x" in done else self.x)

    def outgoing(self, p, k, own=None):
        route = self.parts[p][2]
        region = self.held(p, route[:k], self.c)
        source = region if own is None else own
        if route[k] == "z":
            devices = [self.device(z=(self.z + j) % 4) for j in (1, 2, 3)]
        else:
            devices = [self.device(y=1 - self.y) if route[k] == "y" else self.device(x=1 - self.x)]
        return [self.remote(source, region, p, k, device) for device in devices]

    def arriving(self, p, k, c):
        route = self.parts[p][2]
        done = route[:k]
        z = ALL if "z" in done else self.z
        y = ALL if "y" in done else self.y
        x = None if "x" in done else self.x
        if route[k] == "z":
            return [self.region(p, (self.z + j) % 4, y, c, x) for j in (1, 2, 3)]
        if route[k] == "y":
            return [self.region(p, z, 1 - self.y, c, x)]
        return [self.region(p, z, y, c, 1 - self.x)]

    def amount(self, p, k):
        route = self.parts[p][2]
        if route[k] != "z":
            return self.held(p, route[:k], self.c)
        y = ALL if "y" in route[:k] else self.y
        return self.region(p, pl.ds(0, 3), y, self.c, None if "x" in route[:k] else self.x)

    def sibling(self, p, k, c):
        regions = [self.held(p, self.parts[p][2][:1], c)] if k == 0 else self.arriving(p, k, c)
        device = self.device(c=1 - self.c)
        return [self.remote(ref, ref, p, 3 + k, device) for ref in regions]

    def sibling_amount(self, p, k):
        ref = self.held(p, self.parts[p][2][:1], self.c) if k == 0 else self.amount(p, k)
        return self.remote(ref, ref, p, 3 + k, self.device(c=1 - self.c))

    def start(self, copies):
        for copy in copies:
            copy.start()

    def begin(self, p):
        self.place_own(p).start()
        self.start(self.outgoing(p, 0, self.shard(p)))

    def event(self, p, k):
        self.stage_amount(p, k).wait_recv()
        if k == 0:
            self.place_own(p).wait()
        if k < 2:
            self.start(self.outgoing(p, k + 1))
        self.start(self.sibling(p, k, self.c))

    def stage_amount(self, p, k):
        ref = self.amount(p, k)
        return self.remote(ref, ref, p, k, self.device(c=1 - self.c))

    def ready(self, p):
        for k in range(3):
            self.sibling_amount(p, k).wait_recv()

    def drain(self):
        for p in range(len(self.parts)):
            for k in range(3):
                self.stage_amount(p, k).wait_send()
                self.sibling_amount(p, k).wait_send()


class Exchange:
    def __init__(self, r, comm, name, index):
        self.comm, self.index = comm, index
        self.pack = getattr(r, "pack_" + name)
        self.swap = getattr(r, "swap_" + name)
        self.mine = getattr(r, "mine_" + name)
        self.terms = getattr(r, "terms_" + name)
        self.sums = getattr(r, "sums_" + name)
        self.send_sem, self.recv_sem = r.sum_send, r.sum_recv
        self.chip = comm.z * 2 + comm.y

    def remote(self, source, target, stage, device):
        return pltpu.make_async_remote_copy(
            source,
            target,
            self.send_sem.at[self.index, stage],
            self.recv_sem.at[self.index, stage],
            device_id=device,
            device_id_type=MESH,
        )

    def fill(self, sources):
        count = self.pack.shape[3]
        tile = 0
        for ref, width in sources:
            for row in range(ref.shape[0] // 8):
                for col in range(width // 128):
                    core, chip, slot = tile // (8 * count), tile // count % 8, tile % count
                    for x in range(2):
                        start = (x * width if ref.shape[1] > width else 0) + 128 * col
                        self.pack[x, core, chip, slot] = ref[8 * row : 8 * row + 8, start : start + 128]
                    tile += 1
        while tile < 16 * count:
            core, chip, slot = tile // (8 * count), tile // count % 8, tile % count
            for x in range(2):
                self.pack[x, core, chip, slot] = jnp.zeros((8, 128), f32)
            tile += 1

    def swap_copy(self):
        c = self.comm.c
        return self.remote(self.pack.at[:, 1 - c], self.swap, 0, self.comm.device(c=1 - c))

    def chip_copies(self):
        own = self.comm.x * 8 + self.chip
        for j in range(1, 16):
            index = (own + j) % 16
            x, chip = index // 8, index % 8
            yield self.remote(self.mine.at[x, chip], self.terms.at[own], 1, (chip * 2 + self.comm.c, x))

    def sum_copies(self):
        own = self.chip * 2 + self.comm.c
        slot = self.sums.at[own]
        for j in range(1, 16):
            yield self.remote(slot, slot, 2, ((own + j) % 16, self.comm.x))

    def all_copies(self, stage):
        ref = (self.terms if stage == 1 else self.sums).at[pl.ds(0, 15)]
        return self.remote(ref, ref, stage, self.comm.device(c=1 - self.comm.c))

    def start(self, sources):
        self.fill(sources)
        self.swap_copy().start()

    def spread(self):
        self.swap_copy().wait_recv()
        comm = self.comm
        for x in range(2):
            for chip in range(8):
                total = self.pack[x, comm.c, chip] + self.swap[x, chip]
                self.mine[x, chip] = total.reshape(self.mine.shape[2:]).astype(bf16)
        for copy in self.chip_copies():
            copy.start()
        self.terms[comm.x * 8 + self.chip] = self.mine[comm.x, self.chip]

    def add(self):
        self.all_copies(1).wait_recv()
        total = self.terms[0].astype(f32)
        for index in range(1, 16):
            total = total + self.terms[index].astype(f32)
        self.sums[self.chip * 2 + self.comm.c] = total.astype(bf16)
        for copy in self.sum_copies():
            copy.start()

    def collect(self):
        self.all_copies(2).wait_recv()

    def drain(self):
        self.swap_copy().wait_send()
        self.all_copies(1).wait_send()
        self.all_copies(2).wait_send()


def exchange_scratch(name, count):
    tiles = (count, 8, 128)
    return {
        "pack_" + name: ((2, 2, 8) + tiles, f32),
        "swap_" + name: ((2, 8) + tiles, f32),
        "mine_" + name: ((2, 8, count // 2, 16, 128), bf16),
        "terms_" + name: ((16, count // 2, 16, 128), bf16),
    }


PARTS = (
    ("embed", None, "zxy"),
    ("wqkv", 0, "zyx"),
    ("wqkv", 1, "zxy"),
    ("wqkv", 2, "zyx"),
    ("wout", None, "zyx"),
    ("wup", 0, "zxy"),
    ("wup", 1, "xzy"),
    ("wup", 2, "zyx"),
    ("wdown", 0, "zyx"),
    ("wdown", 1, "xyz"),
    ("wdown", 2, "zxy"),
)
PLAN = (
    ("b", 0),
    ("b", 1),
    ("b", 2),
    ("b", 3),
    ("b", 4),
    ("b", 5),
    ("b", 6),
    ("b", 7),
    ("b", 8),
    ("b", 9),
    ("b", 10),
    ("s", "prep0"),
    ("s", "prep1"),
    (0, 6),
    (0, 9),
    (0, 0),
    (0, 1),
    (1, 9),
    (1, 0),
    (0, 2),
    (1, 1),
    (0, 3),
    (1, 2),
    (0, 4),
    (2, 0),
    ("s", "pos0"),
    (1, 3),
    (0, 5),
    (2, 1),
    ("s", "pos1"),
    (0, 7),
    (2, 2),
    ("s", "pos2"),
    (2, 3),
    (0, 8),
    ("s", "pos3"),
    (1, 4),
    ("s", "qkv0"),
    ("s", "qkv1"),
    ("s", "qkv2"),
    ("s", "qkv3"),
    (1, 5),
    (0, 10),
    ("s", "qkv4"),
    (1, 7),
    ("s", "attend0.0"),
    ("s", "attend0.1"),
    ("s", "attend1.0"),
    (1, 8),
    ("s", "attend1.1"),
    (2, 4),
    ("s", "attend2.0"),
    ("s", "attend2.1"),
    (1, 6),
    ("s", "attend3.0"),
    (1, 10),
    ("s", "attend3.1"),
    ("s", "attend4.0"),
    (2, 5),
    ("s", "attend4.1"),
    ("s", "attend5.0"),
    ("s", "attend5.1"),
    ("s", "out"),
    (2, 7),
    ("s", "up0"),
    (2, 6),
    ("s", "up1"),
    ("s", "up2"),
    ("s", "up3"),
    (2, 9),
    ("s", "up4"),
    ("s", "up5"),
    (2, 8),
    ("s", "down"),
    ("s", "down0"),
    (2, 10),
    ("s", "down1"),
    ("s", "down2"),
)


STEPS = dict(
    prep0=(prepare_masks, ()),
    prep1=(prepare_factors, ()),
    pos0=(embed_positions, ("embed",)),
    pos1=(functools.partial(project_position, 0, False, "pq_far_t"), (("wqkv", 0),)),
    pos2=(functools.partial(project_position, 1, True, "pk_near_t"), (("wqkv", 1),)),
    pos3=(functools.partial(project_position, 1, False, "pk_far_t"), ()),
    qkv0=(reduce_tokens, ()),
    qkv1=(functools.partial(project_token, 0, "q"), ()),
    qkv2=(functools.partial(project_token, 1, "k"), ()),
    qkv3=(functools.partial(project_token, 2, "v"), (("wqkv", 2),)),
    qkv4=(arrange_heads, ()),
    attend=(attend, ()),
    out=(out_project, ("wout",)),
    up=(up_project, ()),
    down=(down_reduce, ()),
    down0=(functools.partial(down_third, 0), (("wdown", 0),)),
    down1=(functools.partial(down_third, 1), (("wdown", 1),)),
    down2=(functools.partial(down_third, 2), (("wdown", 2),)),
)
BACKWARD = (
    norm_two,
    down_back,
    up_back,
    out_back,
)


def run_plan(r, comm, plan):
    ready = set()
    waiting = []
    turns = {}
    counts = dict(attend=H, up=6)

    def act(items):
        for kind, arg in items:
            if kind == "r":
                comm.ready(arg)
            else:
                comm.event(arg, kind)

    def before(*turn):
        for place, items in turns.items():
            if items and place[1:] == turn[1:]:
                pl.when(turn[0] == place[0])(functools.partial(act, items))

    def need(parts):
        for p, part in enumerate(comm.parts):
            if p not in ready and (part[0] in parts or part[:2] in parts):
                ready.add(p)
                waiting.append(("r", p))

    for kind, arg in plan:
        if kind == "b":
            comm.begin(arg)
            continue
        if kind != "s":
            waiting.append((kind, arg))
            continue
        name = arg.rstrip("0123456789.")
        if name not in counts:
            step, needs = STEPS[arg]
            need(needs)
            act(waiting)
            waiting.clear()
            step(r)
            continue
        turn = tuple(int(c) for c in arg[len(name) :].split("."))
        if name == "up":
            need((("wup", turn[0] // 2),))
        turns[turn] = list(waiting)
        waiting.clear()
        if len(turns) == counts[name]:
            STEPS[name][0](r, before)
            turns = {}
    act(waiting)


EARLY, LATE = 4, 2
SUMS = dict(
    sums_early=((16, EARLY // 2, 16, 128), bf16), sums_late=((16, LATE // 2, 16, 128), bf16)
)
FUSED_SCRATCH = {
    **SCRATCH,
    **GATHERED,
    **GRADS,
    **exchange_scratch("early", EARLY),
    **exchange_scratch("late", LATE),
}


def layer_kernel(fused, *refs):
    r = Refs()
    if fused:
        names = INPUTS + SHARDS + OUTPUTS + list(SUMS) + list(FUSED_SCRATCH)
        names += ["load_sem", "send_sem", "recv_sem", "local_sem", "sum_send", "sum_recv"]
    else:
        names = INPUTS + list(GATHERED) + OUTPUTS + list(GRADS) + list(SCRATCH) + ["load_sem"]
    for name, ref in zip(names, refs, strict=True):
        setattr(r, name, ref)
    for name, target in ALIASES.items():
        setattr(r, name, getattr(r, target))
    if not fused:
        r.grad_lam[...] = jnp.zeros_like(r.grad_lam)
        for step, _ in STEPS.values():
            step(r)
        for step in BACKWARD + (attend_back, qkv_factors, qkv_input, finish_layer, finish_grad):
            step(r)
        return

    comm = Gather(r)
    comm.greet()
    r.grad_lam[...] = jnp.zeros_like(r.grad_lam)
    run_plan(r, comm, PLAN)
    for step in BACKWARD:
        step(r)
    early = Exchange(r, comm, "early", 0)
    late = Exchange(r, comm, "late", 1)
    early.start(((r.grad_wide, FF // 2), (r.grad_narrow, D // 2), (r.grad_fourth, D // 2)))

    def before(p):
        pl.when(p == 1)(early.spread)
        pl.when(p == 4)(early.add)

    attend_back(r, before)
    qkv_factors(r)
    late.start(((r.grad_attn, D // 2), (r.grad_lam, 128)))
    finish_layer(r)
    late.spread()
    qkv_input(r)
    finish_grad(r)
    comm.drain()
    early.collect()
    early.drain()
    late.add()
    late.collect()
    late.drain()


OUT_SHAPES = dict(layer_out=((L, D), bf16), grad_tokens=((L, D), bf16), **SUMS, **GRADS)


def unpack_kernel(layer_in, grad_in, early, late, layer_out, grad_out, ap, aq, upp, upq, dnp, dnq, glam, *parts):
    layer_out[...] = layer_in[...]
    grad_out[...] = grad_in[...]
    wide, narrow, fourth, attn = parts
    for sums, refs in ((early, (wide, narrow, fourth)), (late, (attn,))):
        count = 2 * sums.shape[1]
        tile = 0
        for ref in refs:
            for row in range(ref.shape[0] // 8):
                for col in range(ref.shape[1] // 128):
                    core, chip, slot = tile // (8 * count), tile // count % 8, tile % count
                    pair = sums[chip * 2 + core, slot // 2].astype(f32)
                    half = slice(8 * (slot % 2), 8 * (slot % 2) + 8)
                    ref[8 * row : 8 * row + 8, 128 * col : 128 * col + 128] = pair[half, :]
                    tile += 1
    core, chip, slot = tile // (8 * count), tile // count % 8, tile % count
    lam = sums[chip * 2 + core, slot // 2].astype(f32)[8 * (slot % 2) : 8 * (slot % 2) + 8, :]
    for n in range(4):
        glam[n : n + 1, :] = lam[0:1, R * n : R * (n + 1)]
    glam[4:6, :] = lam[4:6, 0:R]
    upp[...] = wide[:R, :]
    dnq[...] = wide[R:, :]
    upq[...] = narrow[:R, :]
    dnp[...] = narrow[R:, :]
    for n in range(3):
        ap[:, n, :] = attn[R * n : R * (n + 1), :]
        aq[:, n, :] = attn[3 * R + R * n : 3 * R + R * (n + 1), :]
    ap[:, 3, :] = fourth[:R, :]
    aq[:, 3, :] = fourth[R:, :]


def unpack_call(layer_out, grad_tokens, early, late):
    half = D // 2
    vmem = pl.BlockSpec(memory_space=pltpu.VMEM)
    shapes = [
        ((L, D), bf16),
        ((L, D), bf16),
        ((R, 4, half), f32),
        ((R, 4, half), f32),
        ((R, FF // 2), f32),
        ((R, half), f32),
        ((R, half), f32),
        ((R, FF // 2), f32),
        ((6, R), f32),
    ]
    return pl.pallas_call(
        unpack_kernel,
        out_shape=[jax.ShapeDtypeStruct(*shape) for shape in shapes],
        in_specs=[vmem] * 4,
        out_specs=[vmem] * len(shapes),
        scratch_shapes=[
            pltpu.VMEM((2 * R, FF // 2), f32),
            pltpu.VMEM((2 * R, half), f32),
            pltpu.VMEM((2 * R, half), f32),
            pltpu.VMEM((6 * R, half), f32),
        ],
    )(layer_out, grad_tokens, early, late)


def arrange_weight(weight, shape):
    *lead, rows, cols = weight.shape
    if shape[-1] == THIRD:
        split = weight.reshape(rows, 2, 3, THIRD)
        return jnp.transpose(split, (2, 1, 0, 3)).reshape(shape)
    split = weight.reshape(*lead, rows, 2, cols // 2)
    return jnp.moveaxis(split, -2, len(lead)).reshape(shape)


def layer_call(args, weights, fused):
    vmem = pl.BlockSpec(memory_space=pltpu.VMEM)
    hbm = pl.BlockSpec(memory_space=pl.ANY)
    load_sem = pltpu.SemaphoreType.DMA((2,))
    if fused:
        outputs = OUTPUTS + list(SUMS)
        scratch = [pltpu.VMEM(*spec) for spec in FUSED_SCRATCH.values()] + [
            load_sem,
            pltpu.SemaphoreType.DMA((len(PARTS), SLOTS)),
            pltpu.SemaphoreType.DMA((len(PARTS), SLOTS)),
            pltpu.SemaphoreType.DMA((len(PARTS),)),
            pltpu.SemaphoreType.DMA((2, 3)),
            pltpu.SemaphoreType.DMA((2, 3)),
        ]
        extra = dict(collective_id=0, has_side_effects=True)
    else:
        outputs = OUTPUTS + list(GRADS)
        scratch = [pltpu.VMEM(*spec) for spec in SCRATCH.values()] + [load_sem]
        weights = [arrange_weight(w, GATHERED[name][0]) for name, w in zip(GATHERED, weights)]
        extra = {}
    return pl.pallas_call(
        functools.partial(layer_kernel, fused),
        out_shape=[jax.ShapeDtypeStruct(*OUT_SHAPES[name]) for name in outputs],
        in_specs=[hbm if name in IN_HBM else vmem for name in INPUTS]
        + [hbm if fused else vmem] * len(weights),
        out_specs=[vmem] * len(outputs),
        scratch_shapes=scratch,
        compiler_params=pltpu.CompilerParams(vmem_limit_bytes=63 * 2**20, **extra),
    )(*args, *weights)


def gather_plain(w_qkv, w_out, w_up, down_t, rel_embed):
    parts = []
    for shard, rows, cols in (
        (w_qkv, 1, 2),
        (w_out, 0, 1),
        (w_up, 0, 1),
        (down_t, 0, 1),
        (rel_embed, 0, 1),
    ):
        part = lax.all_gather(shard, "inner", axis=cols, tiled=True)
        parts.append(lax.all_gather(part, "group", axis=rows, tiled=True))
    return parts


def reduce_plain(grads):
    shared = [
        lax.psum(lax.psum_scatter(g, "inner", scatter_dimension=1, tiled=True), "group")
        for g in grads[:-1]
    ]
    return shared, lax.psum(grads[-1], ("group", "inner"))


def on_device(
    tokens,
    cotangent,
    segments,
    w_qkv,
    w_out,
    w_up,
    w_down,
    rel_embed,
    attn_bias,
    up_bias,
    down_bias,
    norm_gain,
    norm_bias,
    attn_p,
    attn_q,
    up_p,
    up_q,
    down_p,
    down_q,
    lam,
):
    fused = (lax.axis_size("group"), lax.axis_size("inner")) == (16, 2)
    down_t = jnp.transpose(w_down)
    weights = (w_qkv, w_out, w_up, down_t, rel_embed)
    if not fused:
        weights = gather_plain(*weights)
    args = (
        tokens,
        cotangent,
        segments,
        jnp.asarray(bucket_rows()),
        attn_bias,
        up_bias,
        down_bias,
        norm_gain,
        norm_bias,
        jnp.transpose(attn_p, (2, 1, 0)),
        jnp.transpose(attn_q, (2, 1, 0)),
        up_p.T,
        up_q.T,
        down_p.T,
        down_q.T,
        lam,
    )
    layer_out, grad_tokens, *sums = layer_call(args, weights, fused)
    if fused:
        layer_out, grad_tokens, ap, aq, upp, upq, dnp, dnq, grad_lam = unpack_call(
            layer_out, grad_tokens, *sums
        )
    else:
        (wide, narrow, fourth, attn), lam_sums = reduce_plain(sums)
        by_rank = [attn[R * n : R * (n + 1)] for n in range(6)]
        ap = jnp.stack(by_rank[:3] + [fourth[:R]], axis=1)
        aq = jnp.stack(by_rank[3:] + [fourth[R:]], axis=1)
        upp, dnq, upq, dnp = wide[:R], wide[R:], narrow[:R], narrow[R:]
        grad_lam = jnp.concatenate([lam_sums[0, : 4 * R].reshape(4, R), lam_sums[4:6, :R]], axis=0)
    return (
        layer_out,
        grad_tokens,
        jnp.transpose(ap, (2, 1, 0)),
        jnp.transpose(aq, (2, 1, 0)),
        upp.T,
        upq.T,
        dnp.T,
        dnq.T,
        grad_lam,
    )


def solution(mesh):
    rows = P(("group", "inner"), None)
    return jax.shard_map(
        on_device,
        mesh=mesh,
        in_specs=(
            rows,
            rows,
            rows,
            P(None, "group", "inner"),
            P("group", "inner"),
            P("group", "inner"),
            P("inner", "group"),
            P("group", "inner"),
        )
        + (P(),) * 12,
        out_specs=(
            rows,
            rows,
            P("inner", None, None),
            P("inner", None, None),
            P("inner", None),
            P("inner", None),
            P("inner", None),
            P("inner", None),
            P(),
        ),
        check_vma=False,
    )
```

```python
import functools

import jax
import jax.numpy as jnp
import numpy as np
from jax import lax
from jax.experimental import pallas as pl
from jax.experimental.pallas import tpu as pltpu
from jax.sharding import PartitionSpec as P

D = 768
H = 12
DH = 64
FF = 3072
SPAN = 256
L = 512
R = 12
HALF = L // 2
SCALE = (3.0 * DH) ** (-0.5)
EPS = 1e-07

bf16 = jnp.bfloat16
f32 = jnp.float32


def bucket_values(offsets, span_size):
    middle = span_size // 2
    magnitude = np.abs(offsets)
    inside = magnitude <= middle
    clipped = np.maximum(magnitude, middle) * 1.0
    logged = (
        np.ceil(np.log(clipped / middle) / np.log((2 * span_size - 1) / middle) * (middle - 1))
        + middle
    )
    bucket = np.where(inside, offsets, np.sign(offsets) * logged.astype(np.int32))
    return np.clip(bucket + span_size, 0, 2 * span_size - 1).astype(np.int32)


def bucket_rows():
    offsets = np.minimum(np.arange(2 * HALF) - (HALF - 1), HALF - 1)
    far = bucket_values(offsets, SPAN)
    near = bucket_values(-offsets, SPAN)
    return np.stack([near, far]).astype(np.int32)


def mm(a, b):
    return lax.dot_general(a, b, (((1,), (0,)), ((), ())), preferred_element_type=f32)


def mm_t(a, b):
    return lax.dot_general(a, b, (((1,), (1,)), ((), ())), preferred_element_type=f32)


def tmm(a, b):
    return lax.dot_general(a, b, (((0,), (0,)), ((), ())), preferred_element_type=f32)


def iota(shape, dim):
    return lax.broadcasted_iota(jnp.int32, shape, dim)


def loop(count, body):
    def step(index, carry):
        body(index)
        return carry

    lax.fori_loop(0, count, step, 0)


def block(index, size):
    return pl.ds(pl.multiple_of(index * size, size), size)


def mean_row(values):
    return jnp.sum(values, axis=1, keepdims=True) * (1.0 / D)


def flat(block):
    return block.reshape(-1, block.shape[-1])


def whole(ref):
    return jnp.concatenate([flat(ref[x]) for x in range(2)], axis=1)


THIRD = FF // 6


def whole_wide(ref):
    return jnp.concatenate([flat(ref[t, x]) for x in range(2) for t in range(3)], axis=1)


def third(t, x):
    return pl.ds(pl.multiple_of((3 * x + t) * THIRD, THIRD), THIRD)


SCRATCH = dict(
    shift=((L, L), bf16),
    unshift=((L, L), bf16),
    flip=((HALF, HALF), bf16),
    mask=((2, HALF, HALF), f32),
    tok=((L, D), bf16),
    cot=((L, D), bf16),
    pk_near_t=((D, L), bf16),
    pk_far_t=((D, L), bf16),
    pq_far_t=((D, L), bf16),
    emb_near=((L, D), bf16),
    emb_far=((L, D), bf16),
    q=((L, D), bf16),
    k=((L, D), bf16),
    v=((L, D), bf16),
    qt=((D, L), bf16),
    kt=((D, L), bf16),
    k_rev_t=((D, L), bf16),
    g_t=((D, L), bf16),
    v_rev=((L, D), bf16),
    v_rev_t=((D, L), bf16),
    probs=((H, L, HALF), bf16),
    probs_t=((H, L, HALF), bf16),
    ctx=((L, D), bf16),
    attn_pt=((4 * R, D), bf16),
    attn_qt=((4 * R, D), bf16),
    up_pt=((R, FF), bf16),
    up_qt=((R, D), bf16),
    down_pt=((R, D), bf16),
    down_qt=((R, FF), bf16),
    lam_row=((8, 4 * R), f32),
    lam_col=((4 * R, 1), f32),
    up_row=((1, FF), f32),
    down_row=((1, D), f32),
    u_t=((4 * R, L), f32),
    du_t=((4 * R, L), bf16),
    u_pos_t=((4 * R, L), f32),
    u_up_t=((R, L), f32),
    u_down_t=((R, L), f32),
    xhat1=((L, D), f32),
    rs1=((L, 1), f32),
    hidden=((L, D), f32),
    hid=((L, D), bf16),
    act=((L, FF), bf16),
    slope=((L, FF), bf16),
    branch=((L, D), f32),
    gsum2=((L, D), f32),
    gb5=((L, D), bf16),
    gpk_t=((D, L), bf16),
    gpq_t=((D, L), bf16),
)

GATHERED = dict(
    wqkv=((3, 2, 4, 2, 2, 48, D // 2), bf16),
    wout=((2, 4, 2, 2, 48, D // 2), bf16),
    wup=((3, 2, 4, 2, 2, 48, THIRD), bf16),
    wdown=((3, 2, 4, 2, 2, 48, THIRD), bf16),
    embed=((2, 4, 2, 2, 32, D // 2), bf16),
)

ALIASES = dict(
    gpre="slope",
    gsum1="gsum2",
    gb3="gb5",
    gctx="q",
    gq_t="kt",
    gk_t="pk_near_t",
    gv_t="v_rev_t",
    low_out="layer_out",
)

INPUTS = [
    "tokens",
    "cotangent",
    "segments",
    "buckets",
    "attn_bias",
    "up_bias",
    "down_bias",
    "norm_gain",
    "norm_bias",
    "attn_p",
    "attn_q",
    "up_p",
    "up_q",
    "down_p",
    "down_q",
    "lam",
]
SHARDS = [name + "_shard" for name in GATHERED]
IN_HBM = ["tokens", "cotangent"]
OUTPUTS = ["layer_out", "grad_tokens"]
GRADS = dict(
    grad_wide=((2 * R, FF), f32),
    grad_narrow=((2 * R, D), f32),
    grad_fourth=((2 * R, D), f32),
    grad_attn=((6 * R, D), f32),
    grad_lam=((8, 128), f32),
)


class Refs:
    pass


def as_column(row):
    return jnp.transpose(jnp.broadcast_to(row, (128, row.shape[1])))[:, 0:1]


def rank_group(n):
    rank = iota((4 * R, 1), 0)
    return ((rank >= R * n) & (rank < R * (n + 1))).astype(f32)


def prepare_masks(r):
    seg_row = r.segments[...]
    seg_col = as_column(seg_row)
    same = (seg_col == seg_row).astype(f32)
    width = jnp.sum(same, axis=0, keepdims=True)
    place = iota((1, L), 1).astype(f32)
    start = jnp.min(jnp.where(width == float(HALF), place, float(L)), axis=1, keepdims=True)
    row, col = iota((L, L), 0).astype(f32), iota((L, L), 1).astype(f32)
    ahead = row + start
    ahead = jnp.where(ahead >= float(L), ahead - float(L), ahead)
    r.shift[...] = (col == ahead).astype(bf16)
    back = col + start
    back = jnp.where(back >= float(L), back - float(L), back)
    r.unshift[...] = (row == back).astype(bf16)
    r.flip[...] = (iota((HALF, HALF), 0) + iota((HALF, HALF), 1) == HALF - 1).astype(bf16)
    seg_low = jnp.broadcast_to(seg_row.astype(f32), (8, L)).astype(bf16)
    moved_row = mm_t(seg_low, r.shift[...])[0:1, :]
    moved_col = as_column(moved_row)
    for b in range(2):
        rows = slice(HALF * b, HALF * (b + 1))
        r.mask[b] = jnp.where(moved_col[rows, :] == moved_row[:, rows], 0.0, -1e30)


def prepare_factors(r):
    copies = [
        pltpu.make_async_copy(source, target, r.load_sem.at[i])
        for i, (source, target) in enumerate(((r.tokens, r.tok), (r.cotangent, r.cot)))
    ]
    for copy in copies:
        copy.start()
    r.attn_pt[...] = jnp.concatenate([r.attn_p[:, n, :] for n in range(4)], axis=0).astype(bf16)
    r.attn_qt[...] = jnp.concatenate([r.attn_q[:, n, :] for n in range(4)], axis=0).astype(bf16)
    r.up_pt[...] = r.up_p[...].astype(bf16)
    r.up_qt[...] = r.up_q[...].astype(bf16)
    r.down_pt[...] = r.down_p[...].astype(bf16)
    r.down_qt[...] = r.down_q[...].astype(bf16)
    for n in range(4):
        r.lam_row[0:1, R * n : R * (n + 1)] = r.lam[n : n + 1, :]
    r.lam_col[...] = as_column(r.lam_row[0:1, :])
    r.up_row[...] = r.up_bias[...].astype(f32).reshape(1, FF)
    r.down_row[...] = r.down_bias[...].astype(f32).reshape(1, D)
    copies[0].wait()
    r.tok[...] = mm(r.shift[...], r.tok[...]).astype(bf16)
    copies[1].wait()
    r.cot[...] = mm(r.shift[...], r.cot[...]).astype(bf16)


def embed_positions(r):
    column = iota((L, L), 1)
    near_table, far_table = ((as_column(r.buckets[i : i + 1, :]) == column).astype(bf16) for i in range(2))
    r.emb_near[...] = mm(near_table, whole(r.embed)).astype(bf16)
    r.emb_far[...] = mm(far_table, whole(r.embed)).astype(bf16)
    r.u_pos_t[...] = mm_t(r.attn_qt[...], r.emb_far[...])


def project_position(n, near, out, r):
    emb = r.emb_near if near else r.emb_far
    u = mm_t(r.attn_qt[...], emb[...]) if near else r.u_pos_t[...]
    mixed_t = (u * r.lam_col[...] * rank_group(n)).astype(bf16)
    result = (
        mm(emb[...], whole(r.wqkv.at[n]))
        + r.attn_bias[n : n + 1, :].astype(f32)
        + tmm(mixed_t, r.attn_pt[...])
    ).astype(bf16)
    getattr(r, out)[...] = jnp.transpose(result)


def reduce_tokens(r):
    r.u_t[...] = mm_t(r.attn_qt[...], r.tok[...])


def project_token(n, out, r):
    mixed_t = (r.u_t[...] * r.lam_col[...] * rank_group(n)).astype(bf16)
    getattr(r, out)[...] = (
        mm(r.tok[...], whole(r.wqkv.at[n]))
        + r.attn_bias[n : n + 1, :].astype(f32)
        + tmm(mixed_t, r.attn_pt[...])
    ).astype(bf16)


def flip_columns(r, source, target):
    for b in range(2):
        cols = slice(HALF * b, HALF * (b + 1))
        target[:, cols] = mm(source[:, cols], r.flip[...]).astype(bf16)


def arrange_heads(r):
    for b in range(2):
        rows = slice(HALF * b, HALF * (b + 1))
        r.v_rev[rows, :] = mm(r.flip[...], r.v[rows, :]).astype(bf16)
    r.v_rev_t[...] = jnp.transpose(r.v_rev[...])
    r.qt[...] = jnp.transpose(r.q[...])
    r.kt[...] = jnp.transpose(r.k[...])
    flip_columns(r, r.kt, r.k_rev_t)


def head_lanes(a):
    lane = iota((1, 2 * DH), 1)
    return ((lane >= DH) if a else (lane < DH)).astype(bf16)


def attend(r, before=None):
    def pair(p):
        cols = block(p, 2 * DH)
        high = iota((HALF, HALF), 1) + iota((HALF, HALF), 0) >= HALF - 1
        for b in range(2):
            if before is not None:
                before(p, b)
            rows = slice(HALF * b, HALF * (b + 1))
            q, k, v = r.q[rows, cols], r.k[rows, cols], r.v[rows, cols]
            keys = r.kt[cols, rows]
            near_keys, far_queries = r.pk_near_t[cols, :], r.pq_far_t[cols, :]
            probs = []
            for a in range(2):
                lanes = head_lanes(a)
                qa, ka = q * lanes, k * lanes
                content, to, fro = mm(qa, keys), mm(qa, near_keys), mm(ka, far_queries)
                near = jnp.where(high, to[:, :HALF], to[:, HALF:])
                near = pltpu.roll(near, 1, 1, stride=1, stride_axis=0)
                far = jnp.where(high, fro[:, :HALF], fro[:, HALF:])
                far = pltpu.roll(far, 1, 1, stride=1, stride_axis=0)
                scores = (content + near + jnp.transpose(far)) * SCALE + r.mask[b]
                peak = jnp.max(scores, axis=1, keepdims=True)
                terms = jnp.exp(scores - peak)
                total = jnp.sum(terms, axis=1, keepdims=True)
                probs.append((terms * (1.0 / total)).astype(bf16))
            context = mm(probs[0], v * head_lanes(0)) + mm(probs[1], v * head_lanes(1))
            turned = [mm(probs[a], r.flip[...]).astype(bf16) for a in range(2)]
            turned_t = [jnp.transpose(turned[a]) for a in range(2)]
            for a in range(2):
                r.probs[2 * p + a, rows, :] = turned[a]
                r.probs_t[2 * p + a, rows, :] = turned_t[a]
            r.ctx[rows, cols] = context.astype(bf16)

    loop(H // 2, pair)


def out_project(r):
    ctx = r.ctx[...]
    u = mm_t(r.attn_qt[...], ctx)
    r.u_t[3 * R :, :] = u[3 * R :, :]
    mixed_t = (u * r.lam_col[...] * rank_group(3)).astype(bf16)
    r.hidden[...] = (
        mm(ctx, whole(r.wout))
        + r.attn_bias[3:4, :].astype(f32)
        + tmm(mixed_t, r.attn_pt[...])
    )
    gain, bias = r.norm_gain[0:1, :].astype(f32), r.norm_bias[0:1, :].astype(f32)

    def part(i):
        rows = block(i, 128)
        total = r.tok[rows, :].astype(f32) + r.hidden[rows, :]
        centre = total - mean_row(total)
        rs = lax.rsqrt(mean_row(centre * centre) + EPS)
        xhat = centre * rs
        hidden = xhat * gain + bias
        r.xhat1[rows, :] = xhat
        r.rs1[rows, :] = rs
        r.hidden[rows, :] = hidden
        r.hid[rows, :] = hidden.astype(bf16)

    loop(L // 128, part)
    r.u_up_t[...] = mm_t(r.up_qt[...], r.hid[...])


def up_project(r, before=None):
    def part(i):
        if before is not None:
            before(i)
        up_block(r, i // 2, i % 2)

    loop(6, part)


def up_block(r, t, x):
    cols = third(t, x)
    mixed_t = (r.u_up_t[...] * as_column(r.lam[4:5, :])).astype(bf16)
    pre = (
        mm(r.hid[...], flat(r.wup[t, x]))
        + r.up_row[:, cols]
        + tmm(mixed_t, r.up_pt[:, cols])
    )
    phi = 0.5 * (1.0 + lax.erf(pre * np.float32(np.sqrt(0.5))))
    r.act[:, cols] = (pre * phi).astype(bf16)
    bell = jnp.exp(-0.5 * pre * pre) * np.float32(1.0 / np.sqrt(2.0 * np.pi))
    r.slope[:, cols] = (phi + pre * bell).astype(bf16)


def down_reduce(r):
    r.u_down_t[...] = mm_t(r.down_qt[...], r.act[...])
    mixed_t = (r.u_down_t[...] * as_column(r.lam[5:6, :])).astype(bf16)
    r.branch[...] = r.down_row[...] + tmm(mixed_t, r.down_pt[...])


def down_third(t, r):
    act = jnp.concatenate([r.act[:, third(t, x)] for x in range(2)], axis=1)
    weight = jnp.concatenate([flat(r.wdown[t, x]) for x in range(2)], axis=1)
    r.branch[...] += mm_t(act, weight)


def norm_two(r):
    gain, bias = r.norm_gain[1:2, :].astype(f32), r.norm_bias[1:2, :].astype(f32)

    def part(i):
        rows = block(i, 256)
        total = r.hidden[rows, :] + r.branch[rows, :]
        centre = total - mean_row(total)
        rs = lax.rsqrt(mean_row(centre * centre) + EPS)
        xhat = centre * rs
        r.low_out[rows, :] = (xhat * gain + bias).astype(bf16)
        e = r.cot[rows, :].astype(f32) * gain
        grad = rs * (e - mean_row(e) - xhat * mean_row(e * xhat))
        r.gsum2[rows, :] = grad
        r.gb5[rows, :] = grad.astype(bf16)

    loop(L // 256, part)


def back_factors(gb, p_t, u_t, lam):
    dmixed = mm_t(p_t, gb)
    return mm((u_t * lam).astype(bf16), gb), (dmixed * lam).astype(bf16), dmixed * u_t


def as_row(column):
    return jnp.transpose(jnp.broadcast_to(column, (column.shape[0], 128)))[0:1, :]


def down_back(r):
    gb = r.gb5[...]
    dp, du, dlam = back_factors(gb, r.down_pt[...], r.u_down_t[...], as_column(r.lam[5:6, :]))
    r.grad_narrow[R:, :] = dp
    r.grad_lam[5:6, 0:R] = as_row(jnp.sum(dlam, axis=1, keepdims=True))[:, 0:R]

    def part(t):
        for x in range(2):
            cols = third(t, x)
            grad = mm(gb, flat(r.wdown[t, x])) + tmm(du, r.down_qt[:, cols])
            r.grad_wide[R:, cols] = mm(du, r.act[:, cols])
            r.gpre[:, cols] = (grad * r.slope[:, cols].astype(f32)).astype(bf16)

    loop(3, part)


def up_back(r):
    gb = r.gpre[...]
    dp, du, dlam = back_factors(gb, r.up_pt[...], r.u_up_t[...], as_column(r.lam[4:5, :]))
    r.grad_wide[:R, :] = dp
    r.grad_lam[4:5, 0:R] = as_row(jnp.sum(dlam, axis=1, keepdims=True))[:, 0:R]
    r.grad_narrow[:R, :] = mm(du, r.hid[...])
    r.branch[...] = mm_t(gb, whole_wide(r.wup)) + tmm(du, r.up_qt[...])
    gain = r.norm_gain[0:1, :].astype(f32)

    def part(i):
        rows = block(i, 256)
        e = (r.gsum2[rows, :] + r.branch[rows, :]) * gain
        xhat = r.xhat1[rows, :]
        grad = r.rs1[rows, :] * (e - mean_row(e) - xhat * mean_row(e * xhat))
        r.gsum1[rows, :] = grad
        r.gb3[rows, :] = grad.astype(bf16)

    loop(L // 256, part)


def out_back(r):
    gb = r.gb3[...]
    dp, du, dlam = back_factors(gb, r.attn_pt[...], r.u_t[...], r.lam_col[...] * rank_group(3))
    r.grad_fourth[:R, :] = dp[3 * R :, :]
    r.grad_fourth[R:, :] = mm(du, r.ctx[...])[3 * R :, :]
    r.grad_lam[0:1, 0 : 4 * R] = as_row(jnp.sum(dlam * rank_group(3), axis=1, keepdims=True))
    r.gctx[...] = (mm_t(gb, whole(r.wout)) + tmm(du, r.attn_qt[...])).astype(bf16)
    r.g_t[...] = jnp.transpose(r.gctx[...])


def attend_back(r, before=None):
    def pair(p):
        if before is not None:
            before(p)
        cols = block(p, 2 * DH)
        low = iota((HALF, HALF), 1) >= iota((HALF, HALF), 0)
        zero = jnp.zeros((HALF, HALF), bf16)
        units = [(a, b) for a in range(2) for b in range(2)]
        part = [slice(HALF * b, HALF * (b + 1)) for b in range(2)]
        feats = [block(2 * p + a, DH) for a in range(2)]
        ready, stores = {}, []
        for a, b in units:
            rows, head, lanes = part[b], 2 * p + a, head_lanes(a)
            gprobs = mm(r.gctx[rows, cols] * lanes, r.v_rev_t[cols, rows])
            gprobs_t = mm(r.v_rev[rows, cols] * lanes, r.g_t[cols, rows])
            probs = r.probs[head, rows, :].astype(f32)
            delta = jnp.sum(probs * gprobs, axis=1, keepdims=True)
            gs = (probs * (gprobs - delta)).astype(bf16)
            probs_t = r.probs_t[head, rows, :].astype(f32)
            delta_t = jnp.sum(probs_t * gprobs_t, axis=0, keepdims=True)
            gs_t = (probs_t * (gprobs_t - delta_t)).astype(bf16)
            ready[a, b] = gs, gs_t
        for a in range(2):
            gpk = gpq = None
            for b in range(2):
                rows = part[b]
                gs, gs_t = ready[a, b]
                turn = pltpu.roll(gs, 0, 1, stride=1, stride_axis=0)
                to = jnp.concatenate([jnp.where(low, turn, zero), jnp.where(low, zero, turn)], axis=1)
                turn_t = pltpu.roll(gs_t, 0, 1, stride=1, stride_axis=0)
                fro = jnp.concatenate([jnp.where(low, turn_t, zero), jnp.where(low, zero, turn_t)], axis=1)
                queries, keys = r.qt[feats[a], rows], r.k_rev_t[feats[a], rows]
                query_part = mm(queries, jnp.concatenate([gs, to], axis=1))
                key_part = mm(keys, jnp.concatenate([gs_t, fro], axis=1))
                gk = query_part[:, :HALF] + mm_t(r.pq_far_t[feats[a], :], fro)
                gv = mm(r.g_t[feats[a], rows], r.probs[2 * p + a, rows, :])
                gq = key_part[:, :HALF] + mm_t(r.pk_far_t[feats[a], :], to)
                gpk_b, gpq_b = query_part[:, HALF:], key_part[:, HALF:]
                gpk = gpk_b if gpk is None else gpk + gpk_b
                gpq = gpq_b if gpq is None else gpq + gpq_b
                stores.append((r.gq_t, feats[a], rows, gq * SCALE))
                stores.append((r.gk_t, feats[a], rows, gk * SCALE))
                stores.append((r.gv_t, feats[a], rows, gv))
            stores.append((r.gpk_t, feats[a], slice(None), gpk * SCALE))
            stores.append((r.gpq_t, feats[a], slice(None), gpq * SCALE))
        for ref, feat, rows, value in stores:
            ref[feat, rows] = value.astype(bf16)

    loop(H // 2, pair)


def qkv_factors(r):
    flip_columns(r, r.gk_t, r.gk_t)
    flip_columns(r, r.gv_t, r.gv_t)
    lam = r.lam_col[...]
    u = r.u_t[...]
    dmixed = jnp.zeros((4 * R, L), f32)
    ap = jnp.zeros((4 * R, D), f32)
    for n, g in ((0, r.gq_t), (1, r.gk_t), (2, r.gv_t)):
        gb = g[...]
        dmixed += mm(r.attn_pt[...], gb) * rank_group(n)
        ap += mm_t((u * lam * rank_group(n)).astype(bf16), gb)
    du = (dmixed * lam).astype(bf16)
    r.du_t[...] = du
    aq = mm(du, r.tok[...])
    lam_grad = dmixed * u
    u = r.u_pos_t[...]
    for n, grads in ((0, r.gpq_t), (1, r.gpk_t)):
        gb = grads[...]
        dmixed = mm(r.attn_pt[...], gb) * rank_group(n)
        ap += mm_t((u * lam * rank_group(n)).astype(bf16), gb)
        aq += mm((dmixed * lam).astype(bf16), r.emb_far[...])
        lam_grad += dmixed * u
    r.grad_attn[: 3 * R, :] = ap[: 3 * R, :]
    r.grad_attn[3 * R :, :] = aq[: 3 * R, :]
    r.grad_lam[0:1, 0 : 4 * R] += as_row(jnp.sum(lam_grad, axis=1, keepdims=True))


def qkv_input(r):
    grad_t = tmm(r.attn_qt[...], r.du_t[...])
    for n, g in ((0, r.gq_t), (1, r.gk_t), (2, r.gv_t)):
        grad_t += mm(whole(r.wqkv.at[n]), g[...])
    r.gsum1[...] += jnp.transpose(grad_t)


def finish_layer(r):
    r.layer_out[...] = mm(r.unshift[...], r.low_out[...]).astype(bf16)


def finish_grad(r):
    r.grad_tokens[...] = mm(r.unshift[...], r.gsum1[...].astype(bf16)).astype(bf16)


MESH = pl.DeviceIdType.MESH
SLOTS = 6
ALL = slice(None)


class Gather:
    def __init__(self, r):
        self.r, self.parts = r, PARTS
        group = lax.axis_index("group")
        self.x = lax.axis_index("inner")
        self.z, self.y, self.c = group // 4, (group // 2) % 2, group % 2

    def device(self, x=None, y=None, z=None, c=None):
        x = self.x if x is None else x
        y = self.y if y is None else y
        z = self.z if z is None else z
        c = self.c if c is None else c
        return ((z * 2 + y) * 2 + c, x)

    def greet(self):
        barrier = pltpu.get_barrier_semaphore()
        partners = [self.device(x=1 - self.x), self.device(y=1 - self.y), self.device(c=1 - self.c)]
        partners += [self.device(z=(self.z + j) % 4) for j in (1, 2, 3)]
        for partner in partners:
            pl.semaphore_signal(barrier, inc=1, device_id=partner, device_id_type=MESH)
        pl.semaphore_wait(barrier, len(partners))

    def region(self, p, z, y, c, x):
        name, lead, _ = self.parts[p]
        ref = getattr(self.r, name)
        ref = ref if lead is None else ref.at[lead]
        return ref.at[ALL if x is None else x, z, y, c]

    def shard(self, p):
        name, lead, _ = self.parts[p]
        ref = getattr(self.r, name + "_shard")
        if lead is None:
            return ref
        return ref.at[lead] if name == "wqkv" else ref.at[:, pl.ds(lead * THIRD, THIRD)]

    def remote(self, source, target, p, slot, device):
        return pltpu.make_async_remote_copy(
            source,
            target,
            self.r.send_sem.at[p, slot],
            self.r.recv_sem.at[p, slot],
            device_id=device,
            device_id_type=MESH,
        )

    def place_own(self, p):
        target = self.region(p, self.z, self.y, self.c, self.x)
        return pltpu.make_async_copy(self.shard(p), target, self.r.local_sem.at[p])

    def held(self, p, done, c):
        z = ALL if "z" in done else self.z
        y = ALL if "y" in done else self.y
        return self.region(p, z, y, c, None if "x" in done else self.x)

    def outgoing(self, p, k, own=None):
        route = self.parts[p][2]
        region = self.held(p, route[:k], self.c)
        source = region if own is None else own
        if route[k] == "z":
            far = self.z // 2
            near = self.z * (1 - 2 * far) + 3 * far
            targets = [(3 * far + (1 - 2 * far) * place) for place in (3, 2, 1 - near)]
            devices = [self.device(z=target) for target in targets]
        else:
            devices = [self.device(y=1 - self.y) if route[k] == "y" else self.device(x=1 - self.x)]
        return [self.remote(source, region, p, k, device) for device in devices]

    def arriving(self, p, k, c):
        route = self.parts[p][2]
        done = route[:k]
        z = ALL if "z" in done else self.z
        y = ALL if "y" in done else self.y
        x = None if "x" in done else self.x
        if route[k] == "z":
            return [self.region(p, (self.z + j) % 4, y, c, x) for j in (1, 2, 3)]
        if route[k] == "y":
            return [self.region(p, z, 1 - self.y, c, x)]
        return [self.region(p, z, y, c, 1 - self.x)]

    def amount(self, p, k):
        route = self.parts[p][2]
        if route[k] != "z":
            return self.held(p, route[:k], self.c)
        y = ALL if "y" in route[:k] else self.y
        return self.region(p, pl.ds(0, 3), y, self.c, None if "x" in route[:k] else self.x)

    def sibling(self, p, k, c):
        regions = [self.held(p, self.parts[p][2][:1], c)] if k == 0 else self.arriving(p, k, c)
        device = self.device(c=1 - self.c)
        return [self.remote(ref, ref, p, 3 + k, device) for ref in regions]

    def sibling_amount(self, p, k):
        ref = self.held(p, self.parts[p][2][:1], self.c) if k == 0 else self.amount(p, k)
        return self.remote(ref, ref, p, 3 + k, self.device(c=1 - self.c))

    def start(self, copies):
        for copy in copies:
            copy.start()

    def begin(self, p):
        self.place_own(p).start()
        self.start(self.outgoing(p, 0, self.shard(p)))

    def event(self, p, k):
        self.stage_amount(p, k).wait_recv()
        if k == 0:
            self.place_own(p).wait()
        if k < 2:
            self.start(self.outgoing(p, k + 1))
        self.start(self.sibling(p, k, self.c))

    def stage_amount(self, p, k):
        ref = self.amount(p, k)
        return self.remote(ref, ref, p, k, self.device(c=1 - self.c))

    def ready(self, p):
        for k in range(3):
            self.sibling_amount(p, k).wait_recv()

    def drain(self):
        for p in range(len(self.parts)):
            for k in range(3):
                self.stage_amount(p, k).wait_send()
                self.sibling_amount(p, k).wait_send()


class Exchange:
    def __init__(self, r, comm, name, index):
        self.comm, self.index = comm, index
        self.pack = getattr(r, "pack_" + name)
        self.swap = getattr(r, "swap_" + name)
        self.mine = getattr(r, "mine_" + name)
        self.terms = getattr(r, "terms_" + name)
        self.sums = getattr(r, "sums_" + name)
        self.send_sem, self.recv_sem = r.sum_send, r.sum_recv
        self.chip = comm.z * 2 + comm.y

    def remote(self, source, target, stage, device):
        return pltpu.make_async_remote_copy(
            source,
            target,
            self.send_sem.at[self.index, stage],
            self.recv_sem.at[self.index, stage],
            device_id=device,
            device_id_type=MESH,
        )

    def fill(self, sources):
        count = self.pack.shape[3]
        tile = 0
        for ref, width in sources:
            for row in range(ref.shape[0] // 8):
                for col in range(width // 128):
                    core, chip, slot = tile // (8 * count), tile // count % 8, tile % count
                    for x in range(2):
                        start = (x * width if ref.shape[1] > width else 0) + 128 * col
                        self.pack[x, core, chip, slot] = ref[8 * row : 8 * row + 8, start : start + 128]
                    tile += 1
        while tile < 16 * count:
            core, chip, slot = tile // (8 * count), tile // count % 8, tile % count
            for x in range(2):
                self.pack[x, core, chip, slot] = jnp.zeros((8, 128), f32)
            tile += 1

    def swap_copy(self):
        c = self.comm.c
        return self.remote(self.pack.at[:, 1 - c], self.swap, 0, self.comm.device(c=1 - c))

    def chip_copies(self):
        own = self.comm.x * 8 + self.chip
        for j in range(1, 16):
            index = (own + j) % 16
            x, chip = index // 8, index % 8
            yield self.remote(self.mine.at[x, chip], self.terms.at[own], 1, (chip * 2 + self.comm.c, x))

    def sum_copies(self):
        own = self.chip * 2 + self.comm.c
        slot = self.sums.at[own]
        for j in range(1, 16):
            yield self.remote(slot, slot, 2, ((own + j) % 16, self.comm.x))

    def all_copies(self, stage):
        ref = (self.terms if stage == 1 else self.sums).at[pl.ds(0, 15)]
        return self.remote(ref, ref, stage, self.comm.device(c=1 - self.comm.c))

    def start(self, sources):
        self.fill(sources)
        self.swap_copy().start()

    def spread(self):
        self.swap_copy().wait_recv()
        comm = self.comm
        for x in range(2):
            for chip in range(8):
                total = self.pack[x, comm.c, chip] + self.swap[x, chip]
                self.mine[x, chip] = total.reshape(self.mine.shape[2:]).astype(bf16)
        for copy in self.chip_copies():
            copy.start()
        self.terms[comm.x * 8 + self.chip] = self.mine[comm.x, self.chip]

    def add(self):
        self.all_copies(1).wait_recv()
        total = self.terms[0].astype(f32)
        for index in range(1, 16):
            total = total + self.terms[index].astype(f32)
        self.sums[self.chip * 2 + self.comm.c] = total.astype(bf16)
        for copy in self.sum_copies():
            copy.start()

    def collect(self):
        self.all_copies(2).wait_recv()

    def drain(self):
        self.swap_copy().wait_send()
        self.all_copies(1).wait_send()
        self.all_copies(2).wait_send()


def exchange_scratch(name, count):
    tiles = (count, 8, 128)
    return {
        "pack_" + name: ((2, 2, 8) + tiles, f32),
        "swap_" + name: ((2, 8) + tiles, f32),
        "mine_" + name: ((2, 8, count // 2, 16, 128), bf16),
        "terms_" + name: ((16, count // 2, 16, 128), bf16),
    }


PARTS = (
    ("embed", None, "zxy"),
    ("wqkv", 0, "zyx"),
    ("wqkv", 1, "zxy"),
    ("wqkv", 2, "zyx"),
    ("wout", None, "zyx"),
    ("wup", 0, "zxy"),
    ("wup", 1, "xzy"),
    ("wup", 2, "zyx"),
    ("wdown", 0, "zyx"),
    ("wdown", 1, "xyz"),
    ("wdown", 2, "zxy"),
)
PLAN = (
    ("b", 0),
    ("b", 1),
    ("b", 2),
    ("b", 3),
    ("b", 4),
    ("b", 5),
    ("b", 6),
    ("b", 7),
    ("b", 8),
    ("b", 9),
    ("b", 10),
    ("s", "prep0"),
    ("s", "prep1"),
    (0, 6),
    (0, 9),
    (0, 0),
    (0, 1),
    (1, 9),
    (1, 0),
    (0, 2),
    (1, 1),
    (0, 3),
    (1, 2),
    (0, 4),
    (2, 0),
    ("s", "pos0"),
    (1, 3),
    (0, 5),
    (2, 1),
    ("s", "pos1"),
    (0, 7),
    (2, 2),
    ("s", "pos2"),
    (2, 3),
    (0, 8),
    ("s", "pos3"),
    (1, 4),
    ("s", "qkv0"),
    ("s", "qkv1"),
    ("s", "qkv2"),
    ("s", "qkv3"),
    (1, 5),
    (0, 10),
    ("s", "qkv4"),
    (1, 7),
    ("s", "attend0.0"),
    ("s", "attend0.1"),
    ("s", "attend1.0"),
    (1, 8),
    ("s", "attend1.1"),
    (2, 4),
    ("s", "attend2.0"),
    ("s", "attend2.1"),
    (1, 6),
    ("s", "attend3.0"),
    (1, 10),
    ("s", "attend3.1"),
    ("s", "attend4.0"),
    (2, 5),
    ("s", "attend4.1"),
    ("s", "attend5.0"),
    ("s", "attend5.1"),
    ("s", "out"),
    (2, 7),
    ("s", "up0"),
    (2, 6),
    ("s", "up1"),
    ("s", "up2"),
    ("s", "up3"),
    (2, 9),
    ("s", "up4"),
    ("s", "up5"),
    (2, 8),
    ("s", "down"),
    ("s", "down0"),
    (2, 10),
    ("s", "down1"),
    ("s", "down2"),
)


STEPS = dict(
    prep0=(prepare_masks, ()),
    prep1=(prepare_factors, ()),
    pos0=(embed_positions, ("embed",)),
    pos1=(functools.partial(project_position, 0, False, "pq_far_t"), (("wqkv", 0),)),
    pos2=(functools.partial(project_position, 1, True, "pk_near_t"), (("wqkv", 1),)),
    pos3=(functools.partial(project_position, 1, False, "pk_far_t"), ()),
    qkv0=(reduce_tokens, ()),
    qkv1=(functools.partial(project_token, 0, "q"), ()),
    qkv2=(functools.partial(project_token, 1, "k"), ()),
    qkv3=(functools.partial(project_token, 2, "v"), (("wqkv", 2),)),
    qkv4=(arrange_heads, ()),
    attend=(attend, ()),
    out=(out_project, ("wout",)),
    up=(up_project, ()),
    down=(down_reduce, ()),
    down0=(functools.partial(down_third, 0), (("wdown", 0),)),
    down1=(functools.partial(down_third, 1), (("wdown", 1),)),
    down2=(functools.partial(down_third, 2), (("wdown", 2),)),
)
BACKWARD = (
    norm_two,
    down_back,
    up_back,
    out_back,
)


def run_plan(r, comm, plan):
    ready = set()
    waiting = []
    turns = {}
    counts = dict(attend=H, up=6)

    def act(items):
        for kind, arg in items:
            if kind == "r":
                comm.ready(arg)
            else:
                comm.event(arg, kind)

    def before(*turn):
        for place, items in turns.items():
            if items and place[1:] == turn[1:]:
                pl.when(turn[0] == place[0])(functools.partial(act, items))

    def need(parts):
        for p, part in enumerate(comm.parts):
            if p not in ready and (part[0] in parts or part[:2] in parts):
                ready.add(p)
                waiting.append(("r", p))

    for kind, arg in plan:
        if kind == "b":
            comm.begin(arg)
            continue
        if kind != "s":
            waiting.append((kind, arg))
            continue
        name = arg.rstrip("0123456789.")
        if name not in counts:
            step, needs = STEPS[arg]
            need(needs)
            act(waiting)
            waiting.clear()
            step(r)
            continue
        turn = tuple(int(c) for c in arg[len(name) :].split("."))
        if name == "up":
            need((("wup", turn[0] // 2),))
        turns[turn] = list(waiting)
        waiting.clear()
        if len(turns) == counts[name]:
            STEPS[name][0](r, before)
            turns = {}
    act(waiting)


EARLY, LATE = 4, 2
SUMS = dict(
    sums_early=((16, EARLY // 2, 16, 128), bf16), sums_late=((16, LATE // 2, 16, 128), bf16)
)
FUSED_SCRATCH = {
    **SCRATCH,
    **GATHERED,
    **GRADS,
    **exchange_scratch("early", EARLY),
    **exchange_scratch("late", LATE),
}


def layer_kernel(fused, *refs):
    r = Refs()
    if fused:
        names = INPUTS + SHARDS + OUTPUTS + list(SUMS) + list(FUSED_SCRATCH)
        names += ["load_sem", "send_sem", "recv_sem", "local_sem", "sum_send", "sum_recv"]
    else:
        names = INPUTS + list(GATHERED) + OUTPUTS + list(GRADS) + list(SCRATCH) + ["load_sem"]
    for name, ref in zip(names, refs, strict=True):
        setattr(r, name, ref)
    for name, target in ALIASES.items():
        setattr(r, name, getattr(r, target))
    if not fused:
        r.grad_lam[...] = jnp.zeros_like(r.grad_lam)
        for step, _ in STEPS.values():
            step(r)
        for step in BACKWARD + (attend_back, qkv_factors, qkv_input, finish_layer, finish_grad):
            step(r)
        return

    comm = Gather(r)
    comm.greet()
    r.grad_lam[...] = jnp.zeros_like(r.grad_lam)
    run_plan(r, comm, PLAN)
    for step in BACKWARD:
        step(r)
    early = Exchange(r, comm, "early", 0)
    late = Exchange(r, comm, "late", 1)
    early.start(((r.grad_wide, FF // 2), (r.grad_narrow, D // 2), (r.grad_fourth, D // 2)))

    def before(p):
        pl.when(p == 1)(early.spread)
        pl.when(p == 4)(early.add)

    attend_back(r, before)
    qkv_factors(r)
    late.start(((r.grad_attn, D // 2), (r.grad_lam, 128)))
    finish_layer(r)
    late.spread()
    qkv_input(r)
    finish_grad(r)
    comm.drain()
    early.collect()
    early.drain()
    late.add()
    late.collect()
    late.drain()


OUT_SHAPES = dict(layer_out=((L, D), bf16), grad_tokens=((L, D), bf16), **SUMS, **GRADS)


def unpack_kernel(layer_in, grad_in, early, late, layer_out, grad_out, ap, aq, upp, upq, dnp, dnq, glam, *parts):
    layer_out[...] = layer_in[...]
    grad_out[...] = grad_in[...]
    wide, narrow, fourth, attn = parts
    for sums, refs in ((early, (wide, narrow, fourth)), (late, (attn,))):
        count = 2 * sums.shape[1]
        tile = 0
        for ref in refs:
            for row in range(ref.shape[0] // 8):
                for col in range(ref.shape[1] // 128):
                    core, chip, slot = tile // (8 * count), tile // count % 8, tile % count
                    pair = sums[chip * 2 + core, slot // 2].astype(f32)
                    half = slice(8 * (slot % 2), 8 * (slot % 2) + 8)
                    ref[8 * row : 8 * row + 8, 128 * col : 128 * col + 128] = pair[half, :]
                    tile += 1
    core, chip, slot = tile // (8 * count), tile // count % 8, tile % count
    lam = sums[chip * 2 + core, slot // 2].astype(f32)[8 * (slot % 2) : 8 * (slot % 2) + 8, :]
    for n in range(4):
        glam[n : n + 1, :] = lam[0:1, R * n : R * (n + 1)]
    glam[4:6, :] = lam[4:6, 0:R]
    upp[...] = wide[:R, :]
    dnq[...] = wide[R:, :]
    upq[...] = narrow[:R, :]
    dnp[...] = narrow[R:, :]
    for n in range(3):
        ap[:, n, :] = attn[R * n : R * (n + 1), :]
        aq[:, n, :] = attn[3 * R + R * n : 3 * R + R * (n + 1), :]
    ap[:, 3, :] = fourth[:R, :]
    aq[:, 3, :] = fourth[R:, :]


def unpack_call(layer_out, grad_tokens, early, late):
    half = D // 2
    vmem = pl.BlockSpec(memory_space=pltpu.VMEM)
    shapes = [
        ((L, D), bf16),
        ((L, D), bf16),
        ((R, 4, half), f32),
        ((R, 4, half), f32),
        ((R, FF // 2), f32),
        ((R, half), f32),
        ((R, half), f32),
        ((R, FF // 2), f32),
        ((6, R), f32),
    ]
    return pl.pallas_call(
        unpack_kernel,
        out_shape=[jax.ShapeDtypeStruct(*shape) for shape in shapes],
        in_specs=[vmem] * 4,
        out_specs=[vmem] * len(shapes),
        scratch_shapes=[
            pltpu.VMEM((2 * R, FF // 2), f32),
            pltpu.VMEM((2 * R, half), f32),
            pltpu.VMEM((2 * R, half), f32),
            pltpu.VMEM((6 * R, half), f32),
        ],
    )(layer_out, grad_tokens, early, late)


def arrange_weight(weight, shape):
    *lead, rows, cols = weight.shape
    if shape[-1] == THIRD:
        split = weight.reshape(rows, 2, 3, THIRD)
        return jnp.transpose(split, (2, 1, 0, 3)).reshape(shape)
    split = weight.reshape(*lead, rows, 2, cols // 2)
    return jnp.moveaxis(split, -2, len(lead)).reshape(shape)


def layer_call(args, weights, fused):
    vmem = pl.BlockSpec(memory_space=pltpu.VMEM)
    hbm = pl.BlockSpec(memory_space=pl.ANY)
    load_sem = pltpu.SemaphoreType.DMA((2,))
    if fused:
        outputs = OUTPUTS + list(SUMS)
        scratch = [pltpu.VMEM(*spec) for spec in FUSED_SCRATCH.values()] + [
            load_sem,
            pltpu.SemaphoreType.DMA((len(PARTS), SLOTS)),
            pltpu.SemaphoreType.DMA((len(PARTS), SLOTS)),
            pltpu.SemaphoreType.DMA((len(PARTS),)),
            pltpu.SemaphoreType.DMA((2, 3)),
            pltpu.SemaphoreType.DMA((2, 3)),
        ]
        extra = dict(collective_id=0, has_side_effects=True)
    else:
        outputs = OUTPUTS + list(GRADS)
        scratch = [pltpu.VMEM(*spec) for spec in SCRATCH.values()] + [load_sem]
        weights = [arrange_weight(w, GATHERED[name][0]) for name, w in zip(GATHERED, weights)]
        extra = {}
    return pl.pallas_call(
        functools.partial(layer_kernel, fused),
        out_shape=[jax.ShapeDtypeStruct(*OUT_SHAPES[name]) for name in outputs],
        in_specs=[hbm if name in IN_HBM else vmem for name in INPUTS]
        + [hbm if fused else vmem] * len(weights),
        out_specs=[vmem] * len(outputs),
        scratch_shapes=scratch,
        compiler_params=pltpu.CompilerParams(vmem_limit_bytes=63 * 2**20, **extra),
    )(*args, *weights)


def gather_plain(w_qkv, w_out, w_up, down_t, rel_embed):
    parts = []
    for shard, rows, cols in (
        (w_qkv, 1, 2),
        (w_out, 0, 1),
        (w_up, 0, 1),
        (down_t, 0, 1),
        (rel_embed, 0, 1),
    ):
        part = lax.all_gather(shard, "inner", axis=cols, tiled=True)
        parts.append(lax.all_gather(part, "group", axis=rows, tiled=True))
    return parts


def reduce_plain(grads):
    shared = [
        lax.psum(lax.psum_scatter(g, "inner", scatter_dimension=1, tiled=True), "group")
        for g in grads[:-1]
    ]
    return shared, lax.psum(grads[-1], ("group", "inner"))


def on_device(
    tokens,
    cotangent,
    segments,
    w_qkv,
    w_out,
    w_up,
    w_down,
    rel_embed,
    attn_bias,
    up_bias,
    down_bias,
    norm_gain,
    norm_bias,
    attn_p,
    attn_q,
    up_p,
    up_q,
    down_p,
    down_q,
    lam,
):
    fused = (lax.axis_size("group"), lax.axis_size("inner")) == (16, 2)
    down_t = jnp.transpose(w_down)
    weights = (w_qkv, w_out, w_up, down_t, rel_embed)
    if not fused:
        weights = gather_plain(*weights)
    args = (
        tokens,
        cotangent,
        segments,
        jnp.asarray(bucket_rows()),
        attn_bias,
        up_bias,
        down_bias,
        norm_gain,
        norm_bias,
        jnp.transpose(attn_p, (2, 1, 0)),
        jnp.transpose(attn_q, (2, 1, 0)),
        up_p.T,
        up_q.T,
        down_p.T,
        down_q.T,
        lam,
    )
    layer_out, grad_tokens, *sums = layer_call(args, weights, fused)
    if fused:
        layer_out, grad_tokens, ap, aq, upp, upq, dnp, dnq, grad_lam = unpack_call(
            layer_out, grad_tokens, *sums
        )
    else:
        (wide, narrow, fourth, attn), lam_sums = reduce_plain(sums)
        by_rank = [attn[R * n : R * (n + 1)] for n in range(6)]
        ap = jnp.stack(by_rank[:3] + [fourth[:R]], axis=1)
        aq = jnp.stack(by_rank[3:] + [fourth[R:]], axis=1)
        upp, dnq, upq, dnp = wide[:R], wide[R:], narrow[:R], narrow[R:]
        grad_lam = jnp.concatenate([lam_sums[0, : 4 * R].reshape(4, R), lam_sums[4:6, :R]], axis=0)
    return (
        layer_out,
        grad_tokens,
        jnp.transpose(ap, (2, 1, 0)),
        jnp.transpose(aq, (2, 1, 0)),
        upp.T,
        upq.T,
        dnp.T,
        dnq.T,
        grad_lam,
    )


def solution(mesh):
    rows = P(("group", "inner"), None)
    return jax.shard_map(
        on_device,
        mesh=mesh,
        in_specs=(
            rows,
            rows,
            rows,
            P(None, "group", "inner"),
            P("group", "inner"),
            P("group", "inner"),
            P("inner", "group"),
            P("group", "inner"),
        )
        + (P(),) * 12,
        out_specs=(
            rows,
            rows,
            P("inner", None, None),
            P("inner", None, None),
            P("inner", None),
            P("inner", None),
            P("inner", None),
            P("inner", None),
            P(),
        ),
        check_vma=False,
    )
```
